128 devices in a mesh: tm: 16 (over z, x), obs: 8 (over y, core).
Axes of the slice: x: 4, y: 4, z: 4, core: 2. Of those that a mesh axis runs over, the one named last changes fastest.
Arguments:
- basis: bfloat16 [2048, 128, 512], P(('tm', 'obs')), may hold values from -0.03125 to 0.03125
- obs_weight: float32 [2048, 128], P(('tm', 'obs')), may hold values from 0.2 to 5
- col_pattern: int32 [2048, 4], P(('tm', 'obs')), may hold values from 0 to 1, as said below
- tile_block: int32 [2048], P(('tm', 'obs')), may hold values from 0 to 31, as said below
- spatial_prec: float32 [512, 512], replicated, as said below
- time_coef: float32 [32], replicated, may hold values from 0.9 to 0.98
Outputs:
- sep_factor: float32 [16, 512, 512], P('tm')
The draws below stay inside these ranges and needn't reach their ends.
Inputs may be any that keep to these rules, and one draw needn't show every extreme that they name: `col_pattern`: each tile's row holds at least one 1. `tile_block`: tile k lies in time block (k // 128) * 2 + m for some m from 0 to 1. `spatial_prec`: symmetric positive definite, smallest eigenvalue 0.5 or more.
All inputs are finite; a program needn't handle non-finite values.
Results may differ from the reference program's by a relative error of at most 0.0003.
Values sent between devices are 32-bit elements; how exact they have to be, the bound alone decides.
A program may use at most 128 MiB of HBM per device.

```python
import math
import jax
import jax.numpy as jnp
from jax import lax

B = 512
CT = 128
RT = 128
TB_DEV = 2
BT = 4
NT = 32
TILES_TM = 128
NTILES = 2048
N_TM = 16


def draw_col_pattern(key, part):
    random_bits = jax.random.randint(key, (NTILES, BT), 0, 2)
    tiles = jnp.arange(NTILES)
    column = jnp.arange(BT)
    first_segment = tiles < TILES_TM
    open_bits = jnp.where(first_segment[:, None] | (column[None, :] < BT - 1), random_bits, 0)
    forced_column = jnp.where(first_segment, tiles % BT, tiles % (BT - 1))
    forced = forced_column[:, None] == column[None, :]
    return jnp.where(forced, 1, open_bits).astype(jnp.int32)


def draw_tile_block(key, part):
    tiles = jnp.arange(NTILES)
    owner = tiles // TILES_TM
    within = tiles % TILES_TM
    chosen = jax.random.randint(key, (NTILES,), 0, TB_DEV)
    chosen = jnp.where(within == 0, 0, chosen)
    chosen = jnp.where(within == TILES_TM - 1, TB_DEV - 1, chosen)
    return (owner * TB_DEV + chosen).astype(jnp.int32)


def draw_spatial_prec(key, part):
    factor = jax.random.normal(key, (B, B), jnp.float32)
    product = jnp.dot(factor, factor.T, precision=lax.Precision.HIGHEST) / B
    return product + 0.5 * jnp.eye(B, dtype=jnp.float32)


def block_levels(stream_key, dims, split, least, top_value):
    gain, own = 1.0, jax.random.fold_in(stream_key, 6)
    for dim, blocks in split:
        draws = jnp.exp(jax.random.uniform(jax.random.fold_in(own, dim), (blocks,), jnp.float32, least / len(split), top_value / len(split)))
        gain = gain * jnp.repeat(draws, dims[dim] // blocks).reshape([-1 if axis == dim else 1 for axis in range(len(dims))])
    return gain


def noise(own_key, dims, spread, most, pieces=(), kind=jnp.bfloat16):
    result = jax.random.normal(own_key, dims, jnp.float32) * spread
    if len(pieces) > 0:
        result = block_levels(own_key, dims, pieces, -0.22, 0.18) * result
    return jnp.clip(result, min=-most, max=most).astype(kind)


def setup_inputs(seed: int = 0) -> dict:
    splits = jax.random.split(jax.random.key(seed), 7)
    basis = noise(splits[0], (NTILES, RT, B), (4 * TILES_TM * RT // TB_DEV) ** -0.5, 0.03125, ((0, 128),))
    obs_weight = jnp.clip(jnp.exp(math.log(5.0) - 3.218876 * jax.random.uniform(splits[1], (NTILES, RT), jnp.float32) ** block_levels(splits[1], (NTILES, RT), ((0, 128),), -0.2, 0.2)), 0.2, 5.0)
    col_pattern = draw_col_pattern(jax.random.fold_in(splits[6], 71), 0)
    tile_block = draw_tile_block(jax.random.fold_in(splits[6], 71), 0)
    spatial_prec = draw_spatial_prec(jax.random.fold_in(splits[6], 71), 0)
    time_coef = jnp.clip(jax.random.uniform(splits[5], (NT,), jnp.float32, 0.9, 0.98), 0.9, 0.98)
    return {"basis": basis, "obs_weight": obs_weight, "col_pattern": col_pattern, "tile_block": tile_block, "spatial_prec": spatial_prec, "time_coef": time_coef}


def solve_lower(lower_factor, rhs):
    return lax.linalg.triangular_solve(lower_factor, rhs, left_side=True, lower=True)

def inner_dot(left_part, right_part):
    return jnp.dot(left_part.T, right_part, precision=lax.Precision.HIGHEST)

def eliminate_segment(gram_blocks, decay_rates, prior_rate, spatial_prec):
    columns = spatial_prec.shape[0]
    nblock = gram_blocks.shape[0]
    first_diag = (1.0 + decay_rates[0] * decay_rates[0]) * spatial_prec + gram_blocks[0]
    first_left = -prior_rate * spatial_prec

    def advance(position, state_tuple):
        diagonal, left_block, absorbed = state_tuple
        lower_factor = jnp.linalg.cholesky(diagonal)
        right_block = -decay_rates[position] * spatial_prec
        solved = solve_lower(lower_factor, jnp.concatenate([right_block, left_block.T], axis=1))
        solved_right = solved[:, :columns]
        solved_left = solved[:, columns:]
        rate_next = decay_rates[position + 1]
        following = (1.0 + rate_next * rate_next) * spatial_prec + gram_blocks[position + 1] - inner_dot(solved_right, solved_right)
        return (following, -inner_dot(solved_left, solved_right), absorbed + inner_dot(solved_left, solved_left))
    return lax.fori_loop(0, nblock - 1, advance, (first_diag, first_left, jnp.zeros_like(spatial_prec)))

def reference(basis, obs_weight, col_pattern, tile_block, spatial_prec, time_coef):
    column_mask = jnp.repeat(col_pattern.astype(jnp.float32), CT, axis=1)

    def add_tile(gram_blocks, tile):
        raw = basis[tile].astype(jnp.float32) * column_mask[tile][None, :]
        rounded = (jnp.sqrt(obs_weight[tile])[:, None] * raw).astype(jnp.bfloat16)
        rounded = lax.optimization_barrier(rounded)
        scaled = rounded.astype(jnp.float32)
        return (gram_blocks.at[tile_block[tile]].add(inner_dot(scaled, scaled)), None)
    gram_blocks = lax.scan(add_tile, jnp.zeros((NT, B, B), jnp.float32), jnp.arange(NTILES))[0]

    def segment(segment_index):
        first_block = segment_index * TB_DEV
        decay_rates = lax.dynamic_slice_in_dim(time_coef, first_block, TB_DEV)
        earlier = lax.dynamic_index_in_dim(time_coef, jnp.maximum(first_block - 1, 0), keepdims=False)
        prior_rate = jnp.where(segment_index > 0, earlier, jnp.zeros_like(earlier))
        blocks = lax.dynamic_slice_in_dim(gram_blocks, first_block, TB_DEV)
        return eliminate_segment(blocks, decay_rates, prior_rate, spatial_prec)
    sep_diag, coupling, absorbed = lax.map(segment, jnp.arange(N_TM))
    reduced = []
    for segment_index in range(N_TM):
        if segment_index + 1 < N_TM:
            reduced.append(sep_diag[segment_index] - absorbed[segment_index + 1])
        else:
            reduced.append(sep_diag[segment_index])
    links = [coupling[segment_index] for segment_index in range(N_TM)]
    stride = 1
    while stride < N_TM:
        factors = [jnp.linalg.cholesky(reduced[index]) for index in range(N_TM)]
        next_reduced = []
        next_links = []
        for index in range(N_TM):
            updated = reduced[index]
            new_link = jnp.zeros_like(links[index])
            if index - stride >= 0:
                solved_here = solve_lower(factors[index - stride], links[index])
                solved_prior = solve_lower(factors[index - stride], links[index - stride].T)
                updated = updated - inner_dot(solved_here, solved_here)
                new_link = -inner_dot(solved_prior, solved_here)
            if index + stride < N_TM:
                solved_above = solve_lower(factors[index + stride], links[index + stride].T)
                updated = updated - inner_dot(solved_above, solved_above)
            next_reduced.append(updated)
            next_links.append(new_link)
        reduced = next_reduced
        links = next_links
        stride = stride * 2
    return jnp.stack([jnp.linalg.cholesky(reduced[index]) for index in range(N_TM)])
```

```python
import jax
import jax.numpy as jnp
from jax import lax
from jax.experimental import pallas as pl
from jax.experimental.pallas import tpu as pltpu
from jax.sharding import PartitionSpec as P

CT = 128
TB_DEV = 2
BLK = 128
VMEM_LIMIT = 48 * 1024 * 1024


def from_behind(block, axis, distance):
    devices = range(lax.axis_size(axis))
    route = [(i - distance, i) for i in devices if i - distance in devices]
    return lax.ppermute(block, axis, route)


def sub_bcast(x, k):
    return jnp.broadcast_to(x[k : k + 1, :], (8, BLK))


def lane_bcast(x, c):
    return jnp.broadcast_to(x[:, c : c + 1], (8, BLK))


def inverse_factor(rows):
    lane = lax.broadcasted_iota(jnp.int32, (8, BLK), 1)
    sub = lax.broadcasted_iota(jnp.int32, (8, BLK), 0)
    rows = list(rows)
    groups = BLK // 8
    for g in range(groups):
        own = rows[g]
        cols = [lane_bcast(own, 8 * g + k) for k in range(8)]
        in_panel = (lane >= 8 * g) & (lane < 8 * g + 8)
        eye = (lane - 8 * g == sub).astype(jnp.float32)
        unit = jnp.where(in_panel, eye, own)
        full = unit
        scale = jnp.zeros((8, BLK), jnp.float32)
        for k in range(0, 8, 2):
            b0, b1 = cols[k], cols[k + 1]
            p, q, r = sub_bcast(b0, k), sub_bcast(b0, k + 1), sub_bcast(b1, k + 1)
            det = p * r - q * q
            inv = 1.0 / det
            m0 = (b0 * r - b1 * q) * inv
            m1 = (b1 * p - b0 * q) * inv
            qi = q * inv
            first, second = sub == k, sub == k + 1
            pair = first | second
            f0 = jnp.where(first, -(r * inv), jnp.where(second, qi, m0))
            f1 = jnp.where(first, qi, jnp.where(second, -(p * inv), m1))
            for j in range(k + 2, 8):
                cols[j] = (
                    jnp.where(pair, 0.0, cols[j])
                    - f0 * sub_bcast(cols[j], k)
                    - f1 * sub_bcast(cols[j], k + 1)
                )
            if g < groups - 1:
                full = (
                    jnp.where(pair, 0.0, full)
                    - f0 * sub_bcast(full, k)
                    - f1 * sub_bcast(full, k + 1)
                )
            ip = 1.0 / p
            below = sub > k + 1
            n0 = jnp.where(below, m0, jnp.where(second, q * ip, 0.0))
            n1 = jnp.where(below, m1, 0.0)
            unit = unit - n0 * sub_bcast(unit, k) - n1 * sub_bcast(unit, k + 1)
            scale = jnp.where(
                first, lax.rsqrt(p), jnp.where(second, lax.rsqrt(det * ip), scale)
            )
        rows[g] = unit * scale
        for h in range(g + 1, groups):
            below = rows[h]
            t = [lane_bcast(below, 8 * g + k) * sub_bcast(full, k) for k in range(8)]
            rows[h] = jnp.where(in_panel, 0.0, below) - (
                ((t[0] + t[1]) + (t[2] + t[3])) + ((t[4] + t[5]) + (t[6] + t[7]))
            )
    return rows


def split(x):
    hi = x.astype(jnp.bfloat16)
    return hi, (x - hi.astype(jnp.float32)).astype(jnp.bfloat16)


def as_left(x):
    hi, lo = split(x)
    return jnp.concatenate([hi, lo, hi], axis=1)


def as_right(x):
    hi, lo = split(x)
    return jnp.concatenate([hi, hi, lo], axis=1)


def dot_nt(left, right):
    return lax.dot_general(
        left, right, (((1,), (1,)), ((), ())), preferred_element_type=jnp.float32
    )


def factor_and_solve(z_ref, inv_ref, n):
    lane = lax.broadcasted_iota(jnp.int32, (8, BLK), 1)
    sub = lax.broadcasted_iota(jnp.int32, (8, BLK), 0)
    steps = n // BLK
    for k in range(steps):
        c = k * BLK
        rows = inverse_factor(
            [z_ref[c + 8 * g : c + 8 * g + 8, c : c + BLK] for g in range(BLK // 8)]
        )
        for g, row in enumerate(rows):
            inv_ref[8 * g : 8 * g + 8, :] = jnp.where(lane <= sub + 8 * g, row, 0.0)
        column = dot_nt(as_left(z_ref[c:, c : c + BLK]), as_right(inv_ref[...]))
        z_ref[c:, c : c + BLK] = column
        if k < steps - 1:
            left = as_left(column[BLK:])
            right = as_right(column[BLK : n - c])
            z_ref[c + BLK :, c + BLK :] -= dot_nt(left, right)


def scaled_tiles_gram(basis_ref, weight_ref, pattern_ref, block_ref, out_ref):
    tiles, _, columns = basis_ref.shape
    root = jnp.sqrt(weight_ref[...]).T
    lane = lax.broadcasted_iota(jnp.int32, (1, columns), 1) // CT
    out_ref[...] = jnp.zeros_like(out_ref)
    for t in range(tiles):
        mask = jnp.zeros((1, columns), jnp.float32)
        for j in range(columns // CT):
            mask = jnp.where(lane == j, pattern_ref[t, j].astype(jnp.float32), mask)
        raw = basis_ref[t].astype(jnp.float32) * mask
        x = (root[:, t : t + 1] * raw).astype(jnp.bfloat16)
        gram = lax.dot_general(
            x, x, (((0,), (0,)), ((), ())), preferred_element_type=jnp.float32
        )
        out_ref[lax.rem(block_ref[t], TB_DEV)] += gram


def segment_kernel(a_ref, v_ref, m_ref, z_ref, inv_ref):
    n = a_ref.shape[0]
    z_ref[:n] = a_ref[...]
    z_ref[n:] = v_ref[...]
    factor_and_solve(z_ref, inv_ref, n)
    solved = z_ref[n:]
    m_ref[...] = dot_nt(as_left(solved), as_right(solved))


def level_kernel(where_ref, a_ref, v_ref, out_ref, z_ref, inv_ref):
    n = a_ref.shape[0]
    part = out_ref.shape[0] // 2
    z_ref[:n] = a_ref[...]
    z_ref[n:] = v_ref[...]
    factor_and_solve(z_ref, inv_ref, n)
    start = pl.multiple_of(where_ref[0] * part, part)
    own = jnp.concatenate(
        [z_ref[pl.ds(n + start, part), :], z_ref[pl.ds(2 * n + start, part), :]], axis=0
    )
    out_ref[...] = dot_nt(as_left(own), as_right(z_ref[n:]))


def final_kernel(a_ref, l_ref, z_ref, inv_ref):
    n = a_ref.shape[0]
    z_ref[...] = a_ref[...]
    factor_and_solve(z_ref, inv_ref, n)
    row = lax.broadcasted_iota(jnp.int32, (n, n), 0)
    col = lax.broadcasted_iota(jnp.int32, (n, n), 1)
    l_ref[...] = jnp.where(col <= row, z_ref[...], 0.0)


VMEM = pl.BlockSpec(memory_space=pltpu.VMEM)
SMEM = pl.BlockSpec(memory_space=pltpu.SMEM)


def params():
    return pltpu.CompilerParams(vmem_limit_bytes=VMEM_LIMIT)


def f32(*shape):
    return jax.ShapeDtypeStruct(shape, jnp.float32)


def per_device(basis, obs_weight, col_pattern, tile_block, spatial_prec, time_coef):
    own = lax.axis_index("tm")
    segments = lax.axis_size("tm")
    where = lax.axis_index("obs")
    copies = lax.axis_size("obs")
    n = spatial_prec.shape[0]
    part = n // copies

    grams = pl.pallas_call(
        scaled_tiles_gram,
        out_shape=f32(TB_DEV, n, n),
        in_specs=[VMEM, VMEM, SMEM, SMEM],
        out_specs=VMEM,
        compiler_params=params(),
    )(basis, obs_weight, col_pattern, tile_block)
    grams = lax.psum(grams, "obs")

    first = own * TB_DEV
    last = time_coef.shape[0] - 1

    def coef(index):
        return lax.dynamic_index_in_dim(time_coef, jnp.clip(index, 0, last), keepdims=False)

    rate0, rate1 = coef(first), coef(first + 1)
    prior = jnp.where(own > 0, coef(first - 1), 0.0)
    rate_above = coef(first + 2)

    def scratch(rows):
        return [pltpu.VMEM((rows, n), jnp.float32), pltpu.VMEM((BLK, BLK), jnp.float32)]

    middle = pl.pallas_call(
        segment_kernel,
        out_shape=f32(n, n),
        in_specs=[VMEM, VMEM],
        out_specs=VMEM,
        scratch_shapes=scratch(2 * n),
        compiler_params=params(),
    )((1.0 + rate0 * rate0) * spatial_prec + grams[0], spatial_prec)

    def own_rows(x):
        return lax.dynamic_slice_in_dim(x, where * part, part, 0)

    above = from_behind(own_rows(middle), "tm", -1)
    a_rows = (
        (1.0 + rate1 * rate1) * own_rows(spatial_prec)
        + own_rows(grams[1])
        - (rate0 * rate0) * own_rows(middle)
        - (rate1 * rate1) * above
    )
    a = lax.all_gather(a_rows, "obs", axis=0, tiled=True)
    above = lax.all_gather(above, "obs", axis=0, tiled=True)
    v = jnp.concatenate([-(prior * rate0) * middle, -(rate1 * rate_above) * above], axis=0)

    for height in range(segments.bit_length() - 1):
        stride = 1 << height
        out = pl.pallas_call(
            level_kernel,
            out_shape=f32(2 * part, 2 * n),
            in_specs=[SMEM, VMEM, VMEM],
            out_specs=VMEM,
            scratch_shapes=scratch(3 * n),
            compiler_params=params(),
        )(where[None].astype(jnp.int32), a, v)
        down = from_behind(out[:part, :n], "tm", -stride)
        up = from_behind(out[part:, n:], "tm", stride)
        a_rows = a_rows - down - up
        a = lax.all_gather(a_rows, "obs", axis=0, tiled=True)
        if 2 * stride < segments:
            link = from_behind(-out[:part, n:], "tm", stride)
            link_above = from_behind(-out[part:, :n], "tm", -stride)
            v = jnp.concatenate(
                [
                    lax.all_gather(link, "obs", axis=0, tiled=True),
                    lax.all_gather(link_above, "obs", axis=0, tiled=True),
                ],
                axis=0,
            )

    factor = pl.pallas_call(
        final_kernel,
        out_shape=f32(n, n),
        in_specs=[VMEM],
        out_specs=VMEM,
        scratch_shapes=scratch(n),
        compiler_params=params(),
    )(a)
    return factor[None]


def solution(mesh):
    in_specs = (
        P(("tm", "obs"), None, None),
        P(("tm", "obs"), None),
        P(("tm", "obs"), None),
        P(("tm", "obs")),
        P(),
        P(),
    )
    out_specs = P("tm", None, None)
    return jax.shard_map(
        per_device, mesh=mesh, in_specs=in_specs, out_specs=out_specs, check_vma=False
    )
```

```python
import functools

import jax
import jax.numpy as jnp
from jax import lax
from jax.experimental import pallas as pl
from jax.experimental.pallas import tpu as pltpu
from jax.sharding import PartitionSpec as P

CT = 128
TB_DEV = 2
BLK = 128
VMEM_LIMIT = 48 * 1024 * 1024


def sub_bcast(x, k):
    return jnp.broadcast_to(x[k : k + 1, :], (8, BLK))


def lane_bcast(x, c):
    return jnp.broadcast_to(x[:, c : c + 1], (8, BLK))


def inverse_factor(rows):
    lane = lax.broadcasted_iota(jnp.int32, (8, BLK), 1)
    sub = lax.broadcasted_iota(jnp.int32, (8, BLK), 0)
    rows = list(rows)
    groups = BLK // 8
    for g in range(groups):
        own = rows[g]
        cols = [lane_bcast(own, 8 * g + k) for k in range(8)]
        in_panel = (lane >= 8 * g) & (lane < 8 * g + 8)
        eye = (lane - 8 * g == sub).astype(jnp.float32)
        unit = jnp.where(in_panel, eye, own)
        full = unit
        scale = jnp.zeros((8, BLK), jnp.float32)
        for k in range(0, 8, 2):
            b0, b1 = cols[k], cols[k + 1]
            p, q, r = sub_bcast(b0, k), sub_bcast(b0, k + 1), sub_bcast(b1, k + 1)
            det = p * r - q * q
            inv = 1.0 / det
            m0 = (b0 * r - b1 * q) * inv
            m1 = (b1 * p - b0 * q) * inv
            qi = q * inv
            first, second = sub == k, sub == k + 1
            pair = first | second
            f0 = jnp.where(first, -(r * inv), jnp.where(second, qi, m0))
            f1 = jnp.where(first, qi, jnp.where(second, -(p * inv), m1))
            for j in range(k + 2, 8):
                cols[j] = (
                    jnp.where(pair, 0.0, cols[j])
                    - f0 * sub_bcast(cols[j], k)
                    - f1 * sub_bcast(cols[j], k + 1)
                )
            if g < groups - 1:
                full = (
                    jnp.where(pair, 0.0, full)
                    - f0 * sub_bcast(full, k)
                    - f1 * sub_bcast(full, k + 1)
                )
            ip = 1.0 / p
            below = sub > k + 1
            n0 = jnp.where(below, m0, jnp.where(second, q * ip, 0.0))
            n1 = jnp.where(below, m1, 0.0)
            unit = unit - n0 * sub_bcast(unit, k) - n1 * sub_bcast(unit, k + 1)
            scale = jnp.where(
                first, lax.rsqrt(p), jnp.where(second, lax.rsqrt(det * ip), scale)
            )
        rows[g] = unit * scale
        for h in range(g + 1, groups):
            below = rows[h]
            t = [lane_bcast(below, 8 * g + k) * sub_bcast(full, k) for k in range(8)]
            rows[h] = jnp.where(in_panel, 0.0, below) - (
                ((t[0] + t[1]) + (t[2] + t[3])) + ((t[4] + t[5]) + (t[6] + t[7]))
            )
    return rows


def split(x):
    hi = x.astype(jnp.bfloat16)
    return hi, (x - hi.astype(jnp.float32)).astype(jnp.bfloat16)


def as_left(x):
    hi, lo = split(x)
    return jnp.concatenate([hi, lo, hi], axis=1)


def as_right(x):
    hi, lo = split(x)
    return jnp.concatenate([hi, hi, lo], axis=1)


def dot_nt(left, right):
    return lax.dot_general(
        left, right, (((1,), (1,)), ((), ())), preferred_element_type=jnp.float32
    )


def factor_and_solve(z_ref, inv_ref, n):
    lane = lax.broadcasted_iota(jnp.int32, (8, BLK), 1)
    sub = lax.broadcasted_iota(jnp.int32, (8, BLK), 0)
    steps = n // BLK
    for k in range(steps):
        c = k * BLK
        rows = inverse_factor(
            [z_ref[c + 8 * g : c + 8 * g + 8, c : c + BLK] for g in range(BLK // 8)]
        )
        for g, row in enumerate(rows):
            inv_ref[8 * g : 8 * g + 8, :] = jnp.where(lane <= sub + 8 * g, row, 0.0)
        column = dot_nt(as_left(z_ref[c:, c : c + BLK]), as_right(inv_ref[...]))
        z_ref[c:, c : c + BLK] = column
        if k < steps - 1:
            left = as_left(column[BLK:])
            right = as_right(column[BLK : n - c])
            z_ref[c + BLK :, c + BLK :] -= dot_nt(left, right)


def scaled_tiles_gram(basis_ref, weight_ref, pattern_ref, block_ref, out_ref):
    tiles, _, columns = basis_ref.shape
    root = jnp.sqrt(weight_ref[...]).T
    lane = lax.broadcasted_iota(jnp.int32, (1, columns), 1) // CT
    out_ref[...] = jnp.zeros_like(out_ref)
    for t in range(tiles):
        mask = jnp.zeros((1, columns), jnp.float32)
        for j in range(columns // CT):
            mask = jnp.where(lane == j, pattern_ref[t, j].astype(jnp.float32), mask)
        raw = basis_ref[t].astype(jnp.float32) * mask
        x = (root[:, t : t + 1] * raw).astype(jnp.bfloat16)
        gram = lax.dot_general(
            x, x, (((0,), (0,)), ((), ())), preferred_element_type=jnp.float32
        )
        out_ref[lax.rem(block_ref[t], TB_DEV)] += gram.reshape(out_ref.shape[1:])


def place():
    where = lax.axis_index("obs")
    return lax.axis_index("tm"), where // 2, lax.rem(where, 2)


def enter(devices):
    barrier = pltpu.get_barrier_semaphore()
    for device in devices:
        pl.semaphore_signal(
            barrier, inc=1, device_id=device, device_id_type=pl.DeviceIdType.MESH
        )
    pl.semaphore_wait(barrier, len(devices))


def remote(src, dst, send, recv, device):
    return pltpu.make_async_remote_copy(
        src_ref=src,
        dst_ref=dst,
        send_sem=send,
        recv_sem=recv,
        device_id=device,
        device_id_type=pl.DeviceIdType.MESH,
    )


CHIPS = 4


def near():
    i, y, c = place()
    chips = [(i, lax.rem(y + d, CHIPS) * 2 + c) for d in range(1, CHIPS)]
    return chips, (i, y * 2 + 1 - c)


class Gather:
    def __init__(self, ref, send, recv):
        _, y, c = place()
        chips, other = near()
        own = ref.at[y * 2 + c]
        self.out = [
            remote(own, own, send.at[d], recv.at[d], chips[d]) for d in range(CHIPS - 1)
        ]
        self.cross, self.back = [], []
        for d in range(CHIPS):
            from_chip = lax.rem(y + CHIPS - d, CHIPS) * 2
            mine, theirs = ref.at[from_chip + c], ref.at[from_chip + 1 - c]
            sems = send.at[CHIPS - 1 + d], recv.at[CHIPS - 1 + d]
            self.cross.append(remote(mine, mine, *sems, other))
            self.back.append(remote(theirs, theirs, *sems, other))
        self.arrive = [
            remote(
                ref.at[lax.rem(y + CHIPS - d, CHIPS) * 2 + c],
                ref.at[lax.rem(y + CHIPS - d, CHIPS) * 2 + c],
                send.at[d - 1],
                recv.at[d - 1],
                chips[d - 1],
            )
            for d in range(1, CHIPS)
        ]

    def start(self):
        for copy in self.out:
            copy.start()
        self.cross[0].start()

    def forward(self):
        for d in (1, 3, 2):
            self.arrive[d - 1].wait_recv()
            self.cross[d].start()

    def finish(self):
        for copy in self.out + self.cross:
            copy.wait_send()
        for copy in self.back:
            copy.wait_recv()


def sum_grams_kernel(
    part_ref, first_ref, second_ref, other_ref, sum_ref, got_ref, xs, xr, ss, sr, gs, gr
):
    i, y, c = place()
    chips, other = near()
    enter(chips + [other])
    swap = [
        remote(part_ref.at[t, :, 1 - c], other_ref.at[t], xs.at[t], xr.at[t], other)
        for t in range(TB_DEV)
    ]
    for copy in swap:
        copy.start()
    spread = []
    for t in range(TB_DEV):
        spread.append(
            [
                remote(
                    sum_ref.at[t, lax.rem(y + d, CHIPS)],
                    got_ref.at[t, d - 1],
                    ss.at[t, d - 1],
                    sr.at[t, d - 1],
                    chips[d - 1],
                )
                for d in range(1, CHIPS)
            ]
        )
    gather = Gather(first_ref, gs, gr)

    def total(t):
        for copy in spread[t]:
            copy.wait_recv()
        return (sum_ref[t, y] + got_ref[t, 0]) + (got_ref[t, 1] + got_ref[t, 2])

    swap[0].wait_recv()
    sum_ref[0] = part_ref[0, :, c] + other_ref[0]
    for copy in spread[0]:
        copy.start()
    swap[1].wait_recv()
    sum_ref[1] = part_ref[1, :, c] + other_ref[1]
    first_ref[y * 2 + c] = total(0)
    gather.start()
    for copy in spread[1]:
        copy.start()
    gather.forward()
    second_ref[...] = total(1)
    gather.finish()
    for copy in swap + spread[0] + spread[1]:
        copy.wait_send()


def along(i, distance):
    count = lax.axis_size("tm")
    return lax.rem(i + count + distance, count)


def join_kernel(
    coef_ref, s_ref, m_ref, g_ref, a_ref, above_ref, rows_ref, ds, dr, gs, gr
):
    i, y, c = place()
    chips, other = near()
    o = y * 2 + c
    down = (along(i, -1), o)
    up = (along(i, 1), o)
    enter(chips + [other, down, up])
    copy = remote(m_ref.at[o], above_ref.at[o], ds, dr, down)
    copy.start()
    gather = Gather(a_ref, gs.at[0], gr.at[0])
    gather_above = Gather(above_ref, gs.at[1], gr.at[1])
    rows = coef_ref[0] * s_ref[o] + g_ref[...] + coef_ref[1] * m_ref[o]
    copy.wait_recv()
    rows = rows + coef_ref[2] * above_ref[o]
    rows_ref[...] = rows
    a_ref[o] = rows
    gather.start()
    gather_above.start()
    gather.forward()
    gather_above.forward()
    gather.finish()
    gather_above.finish()
    copy.wait_send()


def exchange_kernel(stride, last, out_ref, old_ref, a_ref, *refs):
    if last:
        got_ref, ds, dr, gs, gr = refs
    else:
        p_ref, q_ref, rows_ref, got_ref, ds, dr, gs, gr = refs
    i, y, c = place()
    chips, other = near()
    o = y * 2 + c
    down = (along(i, -stride), o)
    up = (along(i, stride), o)
    enter(chips + [other, down, up])
    copies = [
        remote(out_ref.at[0], got_ref.at[0], ds.at[0], dr.at[0], down),
        remote(out_ref.at[3], got_ref.at[1], ds.at[1], dr.at[1], up),
    ]
    gathers = [Gather(a_ref, gs.at[0], gr.at[0])]
    if not last:
        copies.append(remote(out_ref.at[1], p_ref.at[o], ds.at[2], dr.at[2], up))
        copies.append(remote(out_ref.at[2], q_ref.at[o], ds.at[3], dr.at[3], down))
        gathers.append(Gather(p_ref, gs.at[1], gr.at[1]))
        gathers.append(Gather(q_ref, gs.at[2], gr.at[2]))
    for copy in copies:
        copy.start()
    copies[0].wait_recv()
    copies[1].wait_recv()
    rows = old_ref[...] - got_ref[0] - got_ref[1]
    a_ref[o] = rows
    gathers[0].start()
    if not last:
        rows_ref[...] = rows
        for copy, gather in zip(copies[2:], gathers[1:]):
            copy.wait_recv()
            gather.start()
    for gather in gathers:
        gather.forward()
    for gather in gathers:
        gather.finish()
    for copy in copies:
        copy.wait_send()


def segment_kernel(coef_ref, s_ref, g_ref, m_ref, z_ref, inv_ref):
    n = s_ref.shape[0]
    z_ref[:n] = coef_ref[0] * s_ref[...] + g_ref[...]
    z_ref[n:] = s_ref[...]
    factor_and_solve(z_ref, inv_ref, n)
    solved = z_ref[n:]
    m_ref[...] = dot_nt(as_left(solved), as_right(solved))


def level_kernel(coef_ref, a_ref, p_ref, q_ref, out_ref, z_ref, inv_ref):
    n = a_ref.shape[0]
    part = out_ref.shape[1]
    z_ref[:n] = a_ref[...]
    z_ref[n : 2 * n] = coef_ref[0] * p_ref[...]
    z_ref[2 * n :] = coef_ref[1] * q_ref[...]
    factor_and_solve(z_ref, inv_ref, n)
    start = pl.multiple_of(lax.axis_index("obs") * part, part)
    own = jnp.concatenate(
        [z_ref[pl.ds(n + start, part), :], z_ref[pl.ds(2 * n + start, part), :]], axis=0
    )
    left = as_left(own)
    with_p = dot_nt(left, as_right(z_ref[n : 2 * n]))
    with_q = dot_nt(left, as_right(z_ref[2 * n :]))
    out_ref[0] = with_p[:part]
    out_ref[1] = -with_q[:part]
    out_ref[2] = -with_p[part:]
    out_ref[3] = with_q[part:]


def final_kernel(a_ref, l_ref, z_ref, inv_ref):
    n = a_ref.shape[0]
    z_ref[...] = a_ref[...]
    factor_and_solve(z_ref, inv_ref, n)
    row = lax.broadcasted_iota(jnp.int32, (n, n), 0)
    col = lax.broadcasted_iota(jnp.int32, (n, n), 1)
    l_ref[...] = jnp.where(col <= row, z_ref[...], 0.0)


VMEM = pl.BlockSpec(memory_space=pltpu.VMEM)
SMEM = pl.BlockSpec(memory_space=pltpu.SMEM)
DMA = pltpu.SemaphoreType.DMA


def f32(*shape):
    return jax.ShapeDtypeStruct(shape, jnp.float32)


def scratch(*shape):
    return pltpu.VMEM(shape, jnp.float32)


def call(kernel, out_shape, in_specs, scratch_shapes=(), collective_id=None):
    extra = {}
    if collective_id is not None:
        extra = dict(collective_id=collective_id, has_side_effects=True)
    return pl.pallas_call(
        kernel,
        out_shape=out_shape,
        in_specs=in_specs,
        out_specs=jax.tree.map(lambda _: VMEM, out_shape),
        scratch_shapes=scratch_shapes,
        compiler_params=pltpu.CompilerParams(vmem_limit_bytes=VMEM_LIMIT, **extra),
    )


def per_device(basis, obs_weight, col_pattern, tile_block, spatial_prec, time_coef):
    own = lax.axis_index("tm")
    segments = lax.axis_size("tm")
    copies = lax.axis_size("obs")
    n = spatial_prec.shape[0]
    part = n // copies
    slabs = f32(copies, part, n)
    rows = f32(part, n)
    hops = 2 * CHIPS - 1

    first = own * TB_DEV
    final = time_coef.shape[0] - 1

    def coef(index):
        return lax.dynamic_index_in_dim(time_coef, jnp.clip(index, 0, final), keepdims=False)

    rate0, rate1 = coef(first), coef(first + 1)
    prior = jnp.where(own > 0, coef(first - 1), 0.0)
    up = jnp.where(own < segments - 1, rate1, 0.0)
    rate_above = coef(first + 2)

    grams = call(
        scaled_tiles_gram,
        f32(TB_DEV, CHIPS, 2, part, n),
        [VMEM, VMEM, SMEM, SMEM],
    )(basis, obs_weight, col_pattern, tile_block)
    gram0, gram1 = call(
        sum_grams_kernel,
        (slabs, rows),
        [VMEM],
        [
            scratch(TB_DEV, CHIPS, part, n),
            scratch(TB_DEV, CHIPS, part, n),
            scratch(TB_DEV, CHIPS - 1, part, n),
            DMA((TB_DEV,)),
            DMA((TB_DEV,)),
            DMA((TB_DEV, CHIPS - 1)),
            DMA((TB_DEV, CHIPS - 1)),
            DMA((hops,)),
            DMA((hops,)),
        ],
        collective_id=1,
    )(grams)

    middle = call(
        segment_kernel,
        f32(n, n),
        [SMEM, VMEM, VMEM],
        [scratch(2 * n, n), scratch(BLK, BLK)],
    )(jnp.stack([1.0 + rate0 * rate0]), spatial_prec, gram0.reshape(n, n))

    a, above, a_rows = call(
        join_kernel,
        (slabs, slabs, rows),
        [SMEM, VMEM, VMEM, VMEM],
        [DMA, DMA, DMA((2, hops)), DMA((2, hops))],
        collective_id=2,
    )(
        jnp.stack([1.0 + rate1 * rate1, -(rate0 * rate0), -(up * up)]),
        spatial_prec.reshape(copies, part, n),
        middle.reshape(copies, part, n),
        gram1,
    )
    p, q = middle, above.reshape(n, n)
    scales = jnp.stack([-(prior * rate0), -(up * rate_above)])

    for height in range(segments.bit_length() - 1):
        stride = 1 << height
        last = 2 * stride >= segments
        out = call(
            level_kernel,
            f32(4, part, n),
            [SMEM, VMEM, VMEM, VMEM],
            [scratch(3 * n, n), scratch(BLK, BLK)],
        )(scales, a.reshape(n, n), p, q)
        moved, arrays = (2, 1) if last else (4, 3)
        result = call(
            functools.partial(exchange_kernel, stride, last),
            (slabs,) if last else (slabs, slabs, slabs, rows),
            [VMEM, VMEM],
            [
                scratch(2, part, n),
                DMA((moved,)),
                DMA((moved,)),
                DMA((arrays, hops)),
                DMA((arrays, hops)),
            ],
            collective_id=3 + height,
        )(out, a_rows)
        a = result[0]
        if not last:
            p, q, a_rows = result[1].reshape(n, n), result[2].reshape(n, n), result[3]
            scales = jnp.ones((2,), jnp.float32)

    factor = call(
        final_kernel,
        f32(n, n),
        [VMEM],
        [scratch(n, n), scratch(BLK, BLK)],
    )(a.reshape(n, n))
    return factor[None]


def solution(mesh):
    in_specs = (
        P(("tm", "obs"), None, None),
        P(("tm", "obs"), None),
        P(("tm", "obs"), None),
        P(("tm", "obs")),
        P(),
        P(),
    )
    out_specs = P("tm", None, None)
    return jax.shard_map(
        per_device, mesh=mesh, in_specs=in_specs, out_specs=out_specs, check_vma=False
    )
```

```python
import functools

import jax
import jax.numpy as jnp
from jax import lax
from jax.experimental import pallas as pl
from jax.experimental.pallas import tpu as pltpu
from jax.sharding import PartitionSpec as P

CT = 128
TB_DEV = 2
BLK = 128
VMEM_LIMIT = 48 * 1024 * 1024


def sub_bcast(x, k):
    return jnp.broadcast_to(x[k : k + 1, :], (8, BLK))


def lane_bcast(x, c):
    return jnp.broadcast_to(x[:, c : c + 1], (8, BLK))


def inverse_factor(rest):
    lane = lax.broadcasted_iota(jnp.int32, (8, BLK), 1)
    sub = lax.broadcasted_iota(jnp.int32, (8, BLK), 0)
    rows = []
    groups = BLK // 8
    for g in range(groups):
        own = rest[:8]
        cols = [lane_bcast(own, 8 * g + k) for k in range(8)]
        in_panel = (lane >= 8 * g) & (lane < 8 * g + 8)
        eye = (lane - 8 * g == sub).astype(jnp.float32)
        unit = jnp.where(in_panel, eye, own)
        full = unit
        scale = jnp.zeros((8, BLK), jnp.float32)
        for k in range(0, 8, 2):
            b0, b1 = cols[k], cols[k + 1]
            p, q, r = sub_bcast(b0, k), sub_bcast(b0, k + 1), sub_bcast(b1, k + 1)
            det = p * r - q * q
            inv = 1.0 / det
            m0 = (b0 * r - b1 * q) * inv
            m1 = (b1 * p - b0 * q) * inv
            qi = q * inv
            first, second = sub == k, sub == k + 1
            pair = first | second
            f0 = jnp.where(first, -(r * inv), jnp.where(second, qi, m0))
            f1 = jnp.where(first, qi, jnp.where(second, -(p * inv), m1))
            for j in range(k + 2, 8):
                cols[j] = (
                    jnp.where(pair, 0.0, cols[j])
                    - f0 * sub_bcast(cols[j], k)
                    - f1 * sub_bcast(cols[j], k + 1)
                )
            if g < groups - 1:
                full = (
                    jnp.where(pair, 0.0, full)
                    - f0 * sub_bcast(full, k)
                    - f1 * sub_bcast(full, k + 1)
                )
            ip = 1.0 / p
            below = sub > k + 1
            n0 = jnp.where(below, m0, jnp.where(second, q * ip, 0.0))
            n1 = jnp.where(below, m1, 0.0)
            unit = unit - n0 * sub_bcast(unit, k) - n1 * sub_bcast(unit, k + 1)
            scale = jnp.where(
                first, lax.rsqrt(p), jnp.where(second, lax.rsqrt(det * ip), scale)
            )
        rows.append(unit * scale)
        if g < groups - 1:
            rest = rest[8:]
            shape = rest.shape
            t = [
                jnp.broadcast_to(rest[:, 8 * g + k : 8 * g + k + 1], shape)
                * jnp.broadcast_to(full[k : k + 1, :], shape)
                for k in range(8)
            ]
            wide = lax.broadcasted_iota(jnp.int32, shape, 1)
            passed = (wide >= 8 * g) & (wide < 8 * g + 8)
            rest = jnp.where(passed, 0.0, rest) - (
                ((t[0] + t[1]) + (t[2] + t[3])) + ((t[4] + t[5]) + (t[6] + t[7]))
            )
    return rows


def split(x):
    hi = x.astype(jnp.bfloat16)
    return hi, (x - hi.astype(jnp.float32)).astype(jnp.bfloat16)


def as_left(x):
    hi, lo = split(x)
    return jnp.concatenate([hi, lo, hi], axis=1)


def as_right(x):
    hi, lo = split(x)
    return jnp.concatenate([hi, hi, lo], axis=1)


def dot_nt(left, right):
    return lax.dot_general(
        left, right, (((1,), (1,)), ((), ())), preferred_element_type=jnp.float32
    )


def factor(z_ref, inv_ref, between=None):
    lane = lax.broadcasted_iota(jnp.int32, (8, BLK), 1)
    sub = lax.broadcasted_iota(jnp.int32, (8, BLK), 0)
    steps = z_ref.shape[0] // BLK
    for k in range(steps):
        c = k * BLK
        rows = inverse_factor(z_ref[c : c + BLK, c : c + BLK])
        for g, row in enumerate(rows):
            inv_ref[k, 8 * g : 8 * g + 8, :] = jnp.where(lane <= sub + 8 * g, row, 0.0)
        column = dot_nt(as_left(z_ref[c:, c : c + BLK]), as_right(inv_ref[k]))
        z_ref[c:, c : c + BLK] = column
        if k < steps - 1:
            below = column[BLK:]
            z_ref[c + BLK :, c + BLK :] -= dot_nt(as_left(below), as_right(below))
        if between is not None:
            between(k)


def solve(v_ref, z_ref, inv_ref):
    steps = z_ref.shape[0] // BLK
    for k in range(steps):
        c = k * BLK
        column = dot_nt(as_left(v_ref[:, c : c + BLK]), as_right(inv_ref[k]))
        v_ref[:, c : c + BLK] = column
        if k < steps - 1:
            v_ref[:, c + BLK :] -= dot_nt(
                as_left(column), as_right(z_ref[c + BLK :, c : c + BLK])
            )


SLOTS = 8
ROWS = 32
WIDE = 640


def split_at(s):
    return (s // 4 + 1) * BLK


def pack(top, bottom, s):
    def piece(w):
        return jnp.concatenate([top[:, :w], bottom[:, : WIDE - w]], axis=1)

    return jnp.where(s < 4, piece(BLK), piece(2 * BLK))


def pack_rows(ref, s):
    top = ref[pl.ds(pl.multiple_of(s * ROWS, ROWS), ROWS), :]
    bottom = ref[pl.ds(pl.multiple_of((2 * SLOTS - 1 - s) * ROWS, ROWS), ROWS), :]
    return pack(top, bottom, s)


def unpack(z_ref, packed_ref):
    for s in range(SLOTS):
        w = split_at(s)
        r = (2 * SLOTS - 1 - s) * ROWS
        z_ref[s * ROWS : (s + 1) * ROWS, :w] = packed_ref[s, :, :w]
        z_ref[r : r + ROWS, : WIDE - w] = packed_ref[s, :, w:]


def scaled_tiles_gram(basis_ref, weight_ref, pattern_ref, block_ref, out_ref):
    tiles, _, columns = basis_ref.shape
    root = jnp.sqrt(weight_ref[...]).T
    lane = lax.broadcasted_iota(jnp.int32, (1, columns), 1) // CT
    out_ref[...] = jnp.zeros_like(out_ref)
    for t in range(tiles):
        mask = jnp.zeros((1, columns), jnp.float32)
        for j in range(columns // CT):
            mask = jnp.where(lane == j, pattern_ref[t, j].astype(jnp.float32), mask)
        raw = basis_ref[t].astype(jnp.float32) * mask
        x = (root[:, t : t + 1] * raw).astype(jnp.bfloat16)
        gram = lax.dot_general(
            x, x, (((0,), (0,)), ((), ())), preferred_element_type=jnp.float32
        )
        m = lax.rem(block_ref[t], TB_DEV)
        for s in range(SLOTS):
            w = split_at(s)
            r = (2 * SLOTS - 1 - s) * ROWS
            out_ref[m, s // 2, s % 2, :, :w] += gram[s * ROWS : (s + 1) * ROWS, :w]
            out_ref[m, s // 2, s % 2, :, w:] += gram[r : r + ROWS, : WIDE - w]


def place():
    where = lax.axis_index("obs")
    return lax.axis_index("tm"), where // 2, lax.rem(where, 2)


def enter(devices):
    barrier = pltpu.get_barrier_semaphore()
    for device in devices:
        pl.semaphore_signal(
            barrier, inc=1, device_id=device, device_id_type=pl.DeviceIdType.MESH
        )
    pl.semaphore_wait(barrier, len(devices))


def remote(src, dst, send, recv, device):
    return pltpu.make_async_remote_copy(
        src_ref=src,
        dst_ref=dst,
        send_sem=send,
        recv_sem=recv,
        device_id=device,
        device_id_type=pl.DeviceIdType.MESH,
    )


CHIPS = 4


def near():
    i, y, c = place()
    chips = [(i, lax.rem(y + d, CHIPS) * 2 + c) for d in range(1, CHIPS)]
    return chips, (i, y * 2 + 1 - c)


class Gather:
    def __init__(self, ref, send, recv):
        _, y, c = place()
        chips, other = near()
        own = ref.at[y * 2 + c]
        self.out = [
            remote(own, own, send.at[d], recv.at[d], chips[d]) for d in range(CHIPS - 1)
        ]
        self.cross, self.back = [], []
        for d in range(CHIPS):
            from_chip = lax.rem(y + CHIPS - d, CHIPS) * 2
            mine, theirs = ref.at[from_chip + c], ref.at[from_chip + 1 - c]
            sems = send.at[CHIPS - 1 + d], recv.at[CHIPS - 1 + d]
            self.cross.append(remote(mine, mine, *sems, other))
            self.back.append(remote(theirs, theirs, *sems, other))
        self.arrive = [
            remote(
                ref.at[lax.rem(y + CHIPS - d, CHIPS) * 2 + c],
                ref.at[lax.rem(y + CHIPS - d, CHIPS) * 2 + c],
                send.at[d - 1],
                recv.at[d - 1],
                chips[d - 1],
            )
            for d in range(1, CHIPS)
        ]

    def start(self):
        for copy in self.out:
            copy.start()
        self.cross[0].start()

    def forward(self):
        for d in (1, 3, 2):
            self.arrive[d - 1].wait_recv()
            self.cross[d].start()

    def finish(self):
        for copy in self.out + self.cross:
            copy.wait_send()
        for copy in self.back:
            copy.wait_recv()


def along(i, distance):
    count = lax.axis_size("tm")
    return lax.rem(i + count + distance, count)


def segment_kernel(
    coef_ref, s_ref, part_ref, m_ref, second_ref,
    first_ref, other_ref, sum_ref, got_ref, z_ref, v_ref, inv_ref, xs, xr, ss, sr, gs, gr,
):
    i, y, c = place()
    chips, other = near()
    enter(chips + [other])
    swap = [
        remote(part_ref.at[t, :, 1 - c], other_ref.at[t], xs.at[t], xr.at[t], other)
        for t in range(TB_DEV)
    ]
    for copy in swap:
        copy.start()
    spread = [
        [
            remote(
                sum_ref.at[t, lax.rem(y + d, CHIPS)],
                got_ref.at[t, d - 1],
                ss.at[t, d - 1],
                sr.at[t, d - 1],
                chips[d - 1],
            )
            for d in range(1, CHIPS)
        ]
        for t in range(TB_DEV)
    ]
    gather = Gather(first_ref, gs, gr)

    def total(t):
        for copy in spread[t]:
            copy.wait_recv()
        return (sum_ref[t, y] + got_ref[t, 0]) + (got_ref[t, 1] + got_ref[t, 2])

    swap[0].wait_recv()
    sum_ref[0] = part_ref[0, :, c] + other_ref[0]
    for copy in spread[0]:
        copy.start()
    swap[1].wait_recv()
    sum_ref[1] = part_ref[1, :, c] + other_ref[1]
    v_ref[...] = s_ref[...]
    first_ref[y * 2 + c] = total(0)
    gather.start()
    gather.forward()
    for copy in spread[1]:
        copy.start()
    gather.finish()
    unpack(z_ref, first_ref)
    z_ref[...] += coef_ref[0] * s_ref[...]

    def between(k):
        if k == 2:
            second_ref[...] = total(1)

    factor(z_ref, inv_ref, between)
    solve(v_ref, z_ref, inv_ref)
    solved = v_ref[...]
    m_ref[...] = dot_nt(as_left(solved), as_right(solved))
    for copy in swap + spread[0] + spread[1]:
        copy.wait_send()


def products(v_ref, sym_ref, link_ref, o):
    n = v_ref.shape[1]
    part = link_ref.shape[1]
    p, q = as_right(v_ref[:n]), as_right(v_ref[n:])

    def rows(first, count):
        return v_ref[pl.ds(pl.multiple_of(first, count), count), :]

    for t, right in enumerate((p, q)):
        top = rows(t * n + o * ROWS, ROWS)
        bottom = rows(t * n + (2 * SLOTS - 1 - o) * ROWS, ROWS)
        both = dot_nt(as_left(jnp.concatenate([top, bottom], axis=0)), right)
        sym_ref[t] = pack(both[:ROWS], both[ROWS:], o)
    for t, right in enumerate((q, p)):
        link_ref[t] = -dot_nt(as_left(rows(t * n + o * part, part)), right)


def first_level_kernel(
    coef_ref, s_ref, m_ref, g_ref, own_ref, sym_ref, link_ref,
    mine_ref, got_ref, a_ref, above_ref, z_ref, v_ref, inv_ref, ds, dr, gs, gr,
):
    i, y, c = place()
    chips, other = near()
    o = y * 2 + c
    n = z_ref.shape[0]
    part = above_ref.shape[1]
    down = (along(i, -1), o)
    up = (along(i, 1), o)
    enter(chips + [other, down, up])
    mine = pack_rows(m_ref, o)
    mine_ref[...] = mine
    own = m_ref.at[pl.ds(pl.multiple_of(o * part, part), part)]
    copies = [
        remote(mine_ref, got_ref, ds.at[0], dr.at[0], down),
        remote(own, above_ref.at[o], ds.at[1], dr.at[1], down),
    ]
    for copy in copies:
        copy.start()
    gather = Gather(a_ref, gs.at[0], gr.at[0])
    gather_above = Gather(above_ref, gs.at[1], gr.at[1])
    rows = coef_ref[0] * pack_rows(s_ref, o) + g_ref[...] + coef_ref[1] * mine
    copies[0].wait_recv()
    rows = rows + coef_ref[2] * got_ref[...]
    own_ref[...] = rows
    a_ref[o] = rows
    gather.start()
    v_ref[:n] = coef_ref[3] * m_ref[...]
    gather.forward()
    copies[1].wait_recv()
    gather_above.start()
    gather.finish()
    unpack(z_ref, a_ref)

    def between(k):
        if k == 2:
            gather_above.forward()

    factor(z_ref, inv_ref, between)
    gather_above.finish()
    v_ref[n:] = coef_ref[4] * above_ref[...].reshape(n, n)
    solve(v_ref, z_ref, inv_ref)
    products(v_ref, sym_ref, link_ref, o)
    for copy in copies:
        copy.wait_send()


def level_kernel(
    stride, old_ref, sym_ref, link_ref, own_ref, next_sym_ref, next_link_ref,
    got_ref, a_ref, p_ref, q_ref, z_ref, v_ref, inv_ref, ds, dr, gs, gr,
):
    i, y, c = place()
    chips, other = near()
    o = y * 2 + c
    n = z_ref.shape[0]
    down = (along(i, -stride), o)
    up = (along(i, stride), o)
    enter(chips + [other, down, up])
    copies = [
        remote(sym_ref.at[0], got_ref.at[0], ds.at[0], dr.at[0], down),
        remote(sym_ref.at[1], got_ref.at[1], ds.at[1], dr.at[1], up),
        remote(link_ref.at[0], p_ref.at[o], ds.at[2], dr.at[2], up),
        remote(link_ref.at[1], q_ref.at[o], ds.at[3], dr.at[3], down),
    ]
    for copy in copies:
        copy.start()
    gather = Gather(a_ref, gs.at[0], gr.at[0])
    links = [Gather(p_ref, gs.at[1], gr.at[1]), Gather(q_ref, gs.at[2], gr.at[2])]
    copies[0].wait_recv()
    copies[1].wait_recv()
    rows = old_ref[...] - got_ref[0] - got_ref[1]
    own_ref[...] = rows
    a_ref[o] = rows
    gather.start()
    gather.forward()
    for copy, link in zip(copies[2:], links):
        copy.wait_recv()
        link.start()
    gather.finish()
    unpack(z_ref, a_ref)

    def between(k):
        if k == 2:
            for link in links:
                link.forward()

    factor(z_ref, inv_ref, between)
    for link in links:
        link.finish()
    v_ref[:n] = p_ref[...].reshape(n, n)
    v_ref[n:] = q_ref[...].reshape(n, n)
    solve(v_ref, z_ref, inv_ref)
    products(v_ref, next_sym_ref, next_link_ref, o)
    for copy in copies:
        copy.wait_send()


def final_kernel(
    stride, old_ref, sym_ref, l_ref, got_ref, a_ref, z_ref, inv_ref, ds, dr, gs, gr
):
    i, y, c = place()
    chips, other = near()
    o = y * 2 + c
    n = z_ref.shape[0]
    down = (along(i, -stride), o)
    up = (along(i, stride), o)
    enter(chips + [other, down, up])
    copies = [
        remote(sym_ref.at[0], got_ref.at[0], ds.at[0], dr.at[0], down),
        remote(sym_ref.at[1], got_ref.at[1], ds.at[1], dr.at[1], up),
    ]
    for copy in copies:
        copy.start()
    gather = Gather(a_ref, gs, gr)
    copies[0].wait_recv()
    copies[1].wait_recv()
    a_ref[o] = old_ref[...] - got_ref[0] - got_ref[1]
    gather.start()
    gather.forward()
    gather.finish()
    unpack(z_ref, a_ref)
    factor(z_ref, inv_ref)
    row = lax.broadcasted_iota(jnp.int32, (n, n), 0)
    col = lax.broadcasted_iota(jnp.int32, (n, n), 1)
    l_ref[...] = jnp.where(col <= row, z_ref[...], 0.0)
    for copy in copies:
        copy.wait_send()


VMEM = pl.BlockSpec(memory_space=pltpu.VMEM)
SMEM = pl.BlockSpec(memory_space=pltpu.SMEM)
DMA = pltpu.SemaphoreType.DMA


def f32(*shape):
    return jax.ShapeDtypeStruct(shape, jnp.float32)


def scratch(*shape):
    return pltpu.VMEM(shape, jnp.float32)


def call(kernel, out_shape, in_specs, scratch_shapes=(), collective_id=None):
    extra = {}
    if collective_id is not None:
        extra = dict(collective_id=collective_id, has_side_effects=True)
    return pl.pallas_call(
        kernel,
        out_shape=out_shape,
        in_specs=in_specs,
        out_specs=jax.tree.map(lambda _: VMEM, out_shape),
        scratch_shapes=scratch_shapes,
        compiler_params=pltpu.CompilerParams(vmem_limit_bytes=VMEM_LIMIT, **extra),
    )


def per_device(basis, obs_weight, col_pattern, tile_block, spatial_prec, time_coef):
    own = lax.axis_index("tm")
    segments = lax.axis_size("tm")
    copies = lax.axis_size("obs")
    n = spatial_prec.shape[0]
    part = n // copies
    piece = (ROWS, WIDE)
    hops = 2 * CHIPS - 1

    first = own * TB_DEV
    final = time_coef.shape[0] - 1

    def coef(index):
        return lax.dynamic_index_in_dim(time_coef, jnp.clip(index, 0, final), keepdims=False)

    rate0, rate1 = coef(first), coef(first + 1)
    prior = jnp.where(own > 0, coef(first - 1), 0.0)
    up = jnp.where(own < segments - 1, rate1, 0.0)
    rate_above = coef(first + 2)

    grams = call(
        scaled_tiles_gram,
        f32(TB_DEV, CHIPS, 2, *piece),
        [VMEM, VMEM, SMEM, SMEM],
    )(basis, obs_weight, col_pattern, tile_block)
    blocks = scratch(n // BLK, BLK, BLK)
    middle, gram1 = call(
        segment_kernel,
        (f32(n, n), f32(*piece)),
        [SMEM, VMEM, VMEM],
        [
            scratch(SLOTS, *piece),
            scratch(TB_DEV, CHIPS, *piece),
            scratch(TB_DEV, CHIPS, *piece),
            scratch(TB_DEV, CHIPS - 1, *piece),
            scratch(n, n),
            scratch(n, n),
            blocks,
            DMA((TB_DEV,)),
            DMA((TB_DEV,)),
            DMA((TB_DEV, CHIPS - 1)),
            DMA((TB_DEV, CHIPS - 1)),
            DMA((hops,)),
            DMA((hops,)),
        ],
        collective_id=1,
    )(jnp.stack([1.0 + rate0 * rate0]), spatial_prec, grams)

    results = (f32(*piece), f32(2, *piece), f32(2, part, n))
    work = [scratch(n, n), scratch(2 * n, n), blocks]
    slabs = scratch(copies, part, n)
    pieces = scratch(SLOTS, *piece)
    scales = [
        1.0 + rate1 * rate1,
        -(rate0 * rate0),
        -(up * up),
        -(prior * rate0),
        -(up * rate_above),
    ]
    own_piece, sym, link = call(
        first_level_kernel,
        results,
        [SMEM, VMEM, VMEM, VMEM],
        [scratch(*piece), scratch(*piece), pieces, slabs, *work]
        + [DMA((2,)), DMA((2,)), DMA((2, hops)), DMA((2, hops))],
        collective_id=2,
    )(jnp.stack(scales), spatial_prec, middle, gram1)

    stride = 1
    while 2 * stride < segments:
        own_piece, sym, link = call(
            functools.partial(level_kernel, stride),
            results,
            [VMEM, VMEM, VMEM],
            [scratch(2, *piece), pieces, slabs, slabs, *work]
            + [DMA((4,)), DMA((4,)), DMA((3, hops)), DMA((3, hops))],
            collective_id=2 + stride,
        )(own_piece, sym, link)
        stride = 2 * stride

    factor_out = call(
        functools.partial(final_kernel, stride),
        f32(n, n),
        [VMEM, VMEM],
        [scratch(2, *piece), pieces, scratch(n, n), blocks]
        + [DMA((2,)), DMA((2,)), DMA((hops,)), DMA((hops,))],
        collective_id=2 + stride,
    )(own_piece, sym)
    return factor_out[None]


def solution(mesh):
    in_specs = (
        P(("tm", "obs"), None, None),
        P(("tm", "obs"), None),
        P(("tm", "obs"), None),
        P(("tm", "obs")),
        P(),
        P(),
    )
    out_specs = P("tm", None, None)
    return jax.shard_map(
        per_device, mesh=mesh, in_specs=in_specs, out_specs=out_specs, check_vma=False
    )
```

```python
import functools

import jax
import jax.numpy as jnp
from jax import lax
from jax.experimental import pallas as pl
from jax.experimental.pallas import tpu as pltpu
from jax.sharding import PartitionSpec as P

CT = 128
TB_DEV = 2
BLK = 128
VMEM_LIMIT = 48 * 1024 * 1024


def sub_bcast(x, k):
    return jnp.broadcast_to(x[k : k + 1, :], (8, BLK))


def lane_bcast(x, c):
    return jnp.broadcast_to(x[:, c : c + 1], (8, BLK))


def inverse_factor(rest):
    lane = lax.broadcasted_iota(jnp.int32, (8, BLK), 1)
    sub = lax.broadcasted_iota(jnp.int32, (8, BLK), 0)
    rows = []
    groups = BLK // 8
    for g in range(groups):
        own = rest[:8]
        cols = [lane_bcast(own, 8 * g + k) for k in range(8)]
        in_panel = (lane >= 8 * g) & (lane < 8 * g + 8)
        eye = (lane - 8 * g == sub).astype(jnp.float32)
        unit = jnp.where(in_panel, eye, own)
        full = unit
        scale = jnp.zeros((8, BLK), jnp.float32)
        for k in range(0, 8, 2):
            b0, b1 = cols[k], cols[k + 1]
            p, q, r = sub_bcast(b0, k), sub_bcast(b0, k + 1), sub_bcast(b1, k + 1)
            det = p * r - q * q
            inv = 1.0 / det
            m0 = (b0 * r - b1 * q) * inv
            m1 = (b1 * p - b0 * q) * inv
            qi = q * inv
            first, second = sub == k, sub == k + 1
            pair = first | second
            f0 = jnp.where(first, -(r * inv), jnp.where(second, qi, m0))
            f1 = jnp.where(first, qi, jnp.where(second, -(p * inv), m1))
            for j in range(k + 2, 8):
                cols[j] = (
                    jnp.where(pair, 0.0, cols[j])
                    - f0 * sub_bcast(cols[j], k)
                    - f1 * sub_bcast(cols[j], k + 1)
                )
            if g < groups - 1:
                full = (
                    jnp.where(pair, 0.0, full)
                    - f0 * sub_bcast(full, k)
                    - f1 * sub_bcast(full, k + 1)
                )
            ip = 1.0 / p
            below = sub > k + 1
            n0 = jnp.where(below, m0, jnp.where(second, q * ip, 0.0))
            n1 = jnp.where(below, m1, 0.0)
            unit = unit - n0 * sub_bcast(unit, k) - n1 * sub_bcast(unit, k + 1)
            scale = jnp.where(
                first, lax.rsqrt(p), jnp.where(second, lax.rsqrt(det * ip), scale)
            )
        rows.append(unit * scale)
        if g < groups - 1:
            rest = rest[8:]
            shape = rest.shape
            t = [
                jnp.broadcast_to(rest[:, 8 * g + k : 8 * g + k + 1], shape)
                * jnp.broadcast_to(full[k : k + 1, :], shape)
                for k in range(8)
            ]
            wide = lax.broadcasted_iota(jnp.int32, shape, 1)
            passed = (wide >= 8 * g) & (wide < 8 * g + 8)
            rest = jnp.where(passed, 0.0, rest) - (
                ((t[0] + t[1]) + (t[2] + t[3])) + ((t[4] + t[5]) + (t[6] + t[7]))
            )
    return rows


def split(x):
    hi = x.astype(jnp.bfloat16)
    return hi, (x - hi.astype(jnp.float32)).astype(jnp.bfloat16)


def as_left(x):
    hi, lo = split(x)
    return jnp.concatenate([hi, lo, hi], axis=1)


def as_right(x):
    hi, lo = split(x)
    return jnp.concatenate([hi, hi, lo], axis=1)


def dot_nt(left, right):
    return lax.dot_general(
        left, right, (((1,), (1,)), ((), ())), preferred_element_type=jnp.float32
    )


def factor(z_ref, inv_ref, between=None):
    lane = lax.broadcasted_iota(jnp.int32, (8, BLK), 1)
    sub = lax.broadcasted_iota(jnp.int32, (8, BLK), 0)
    steps = z_ref.shape[0] // BLK
    for k in range(steps):
        c = k * BLK
        rows = inverse_factor(z_ref[c : c + BLK, c : c + BLK])
        for g, row in enumerate(rows):
            inv_ref[k, 8 * g : 8 * g + 8, :] = jnp.where(lane <= sub + 8 * g, row, 0.0)
        column = dot_nt(as_left(z_ref[c:, c : c + BLK]), as_right(inv_ref[k]))
        z_ref[c:, c : c + BLK] = column
        if k < steps - 1:
            left, right = as_left(column[BLK:]), as_right(column[BLK:])
            for b in range(c + BLK, z_ref.shape[0], BLK):
                r = b - c - BLK
                z_ref[b:, b : b + BLK] -= dot_nt(left[r:], right[r : r + BLK])
        if between is not None:
            between(k)


def solve_step(v_ref, z_ref, inv_ref, k, first=0):
    c = k * BLK
    column = dot_nt(as_left(v_ref[first:, c : c + BLK]), as_right(inv_ref[k]))
    v_ref[first:, c : c + BLK] = column
    if c + BLK < z_ref.shape[0]:
        v_ref[first:, c + BLK :] -= dot_nt(
            as_left(column), as_right(z_ref[c + BLK :, c : c + BLK])
        )


SLOTS = 8
ROWS = 32
WIDE = 640


def split_at(s):
    return (s // 4 + 1) * BLK


def pack(top, bottom, s):
    def piece(w):
        return jnp.concatenate([top[:, :w], bottom[:, : WIDE - w]], axis=1)

    return jnp.where(s < 4, piece(BLK), piece(2 * BLK))


def pack_rows(ref, s):
    top = ref[pl.ds(pl.multiple_of(s * ROWS, ROWS), ROWS), :]
    bottom = ref[pl.ds(pl.multiple_of((2 * SLOTS - 1 - s) * ROWS, ROWS), ROWS), :]
    return pack(top, bottom, s)


def unpack(z_ref, packed_ref):
    for s in range(SLOTS):
        w = split_at(s)
        r = (2 * SLOTS - 1 - s) * ROWS
        z_ref[s * ROWS : (s + 1) * ROWS, :w] = packed_ref[s, :, :w]
        z_ref[r : r + ROWS, : WIDE - w] = packed_ref[s, :, w:]


def scaled_tiles_gram(basis_ref, weight_ref, pattern_ref, block_ref, out_ref):
    tiles, _, columns = basis_ref.shape
    root = jnp.sqrt(weight_ref[...]).T
    lane = lax.broadcasted_iota(jnp.int32, (1, columns), 1) // CT
    out_ref[...] = jnp.zeros_like(out_ref)
    for t in range(tiles):
        mask = jnp.zeros((1, columns), jnp.float32)
        for j in range(columns // CT):
            mask = jnp.where(lane == j, pattern_ref[t, j].astype(jnp.float32), mask)
        raw = basis_ref[t].astype(jnp.float32) * mask
        x = (root[:, t : t + 1] * raw).astype(jnp.bfloat16)
        gram = lax.dot_general(
            x, x, (((0,), (0,)), ((), ())), preferred_element_type=jnp.float32
        )
        m = lax.rem(block_ref[t], TB_DEV)
        for s in range(SLOTS):
            w = split_at(s)
            r = (2 * SLOTS - 1 - s) * ROWS
            out_ref[m, s // 2, s % 2, :, :w] += gram[s * ROWS : (s + 1) * ROWS, :w]
            out_ref[m, s // 2, s % 2, :, w:] += gram[r : r + ROWS, : WIDE - w]


def place():
    where = lax.axis_index("obs")
    return lax.axis_index("tm"), where // 2, lax.rem(where, 2)


def enter(devices):
    barrier = pltpu.get_barrier_semaphore()
    for device in devices:
        pl.semaphore_signal(
            barrier, inc=1, device_id=device, device_id_type=pl.DeviceIdType.MESH
        )
    pl.semaphore_wait(barrier, len(devices))


def remote(src, dst, send, recv, device):
    return pltpu.make_async_remote_copy(
        src_ref=src,
        dst_ref=dst,
        send_sem=send,
        recv_sem=recv,
        device_id=device,
        device_id_type=pl.DeviceIdType.MESH,
    )


CHIPS = 4


def near():
    i, y, c = place()
    chips = [(i, lax.rem(y + d, CHIPS) * 2 + c) for d in range(1, CHIPS)]
    return chips, (i, y * 2 + 1 - c)


class Gather:
    def __init__(self, ref, send, recv):
        _, y, c = place()
        chips, other = near()
        own = ref.at[y * 2 + c]
        self.out = [
            remote(own, own, send.at[d], recv.at[d], chips[d]) for d in range(CHIPS - 1)
        ]
        self.cross, self.back = [], []
        for d in range(CHIPS):
            from_chip = lax.rem(y + CHIPS - d, CHIPS) * 2
            mine, theirs = ref.at[from_chip + c], ref.at[from_chip + 1 - c]
            sems = send.at[CHIPS - 1 + d], recv.at[CHIPS - 1 + d]
            self.cross.append(remote(mine, mine, *sems, other))
            self.back.append(remote(theirs, theirs, *sems, other))
        self.arrive = [
            remote(
                ref.at[lax.rem(y + CHIPS - d, CHIPS) * 2 + c],
                ref.at[lax.rem(y + CHIPS - d, CHIPS) * 2 + c],
                send.at[d - 1],
                recv.at[d - 1],
                chips[d - 1],
            )
            for d in range(1, CHIPS)
        ]

    def start(self):
        for copy in self.out:
            copy.start()
        self.cross[0].start()

    def forward(self):
        for d in (1, 3, 2):
            self.arrive[d - 1].wait_recv()
            self.cross[d].start()

    def finish(self):
        for copy in self.out + self.cross:
            copy.wait_send()
        for copy in self.back:
            copy.wait_recv()


def rates(coef_ref):
    i, _, _ = place()
    count, last = coef_ref.shape[0], lax.axis_size("tm") - 1
    first = i * TB_DEV
    before = jnp.where(i > 0, coef_ref[lax.rem(first + count - 1, count)], 0.0)
    rate0, rate1 = coef_ref[first], coef_ref[first + 1]
    return before, rate0, rate1, jnp.where(i < last, rate1, 0.0), coef_ref[lax.rem(first + 2, count)]


def along(i, distance):
    count = lax.axis_size("tm")
    return lax.rem(i + count + distance, count)


def segment_kernel(
    coef_ref, s_ref, part_ref, m_ref, second_ref,
    first_ref, other_ref, sum_ref, got_ref, z_ref, v_ref, inv_ref, xs, xr, ss, sr, gs, gr,
):
    i, y, c = place()
    chips, other = near()
    enter(chips + [other])
    swap = [
        remote(part_ref.at[t, :, 1 - c], other_ref.at[t], xs.at[t], xr.at[t], other)
        for t in range(TB_DEV)
    ]
    for copy in swap:
        copy.start()
    spread = [
        [
            remote(
                sum_ref.at[t, lax.rem(y + d, CHIPS)],
                got_ref.at[t, d - 1],
                ss.at[t, d - 1],
                sr.at[t, d - 1],
                chips[d - 1],
            )
            for d in range(1, CHIPS)
        ]
        for t in range(TB_DEV)
    ]
    gather = Gather(first_ref, gs, gr)

    def total(t):
        for copy in spread[t]:
            copy.wait_recv()
        return (sum_ref[t, y] + got_ref[t, 0]) + (got_ref[t, 1] + got_ref[t, 2])

    swap[0].wait_recv()
    sum_ref[0] = part_ref[0, :, c] + other_ref[0]
    for copy in spread[0]:
        copy.start()
    swap[1].wait_recv()
    sum_ref[1] = part_ref[1, :, c] + other_ref[1]
    v_ref[...] = s_ref[...]
    first_ref[y * 2 + c] = total(0)
    gather.start()
    gather.forward()
    for copy in spread[1]:
        copy.start()
    gather.finish()
    unpack(z_ref, first_ref)
    _, rate0, _, _, _ = rates(coef_ref)
    z_ref[...] += (1.0 + rate0 * rate0) * s_ref[...]

    def between(k):
        if k == 2:
            second_ref[...] = total(1)
        solve_step(v_ref, z_ref, inv_ref, k)

    factor(z_ref, inv_ref, between)
    solved = v_ref[...]
    m_ref[...] = dot_nt(as_left(solved), as_right(solved))
    for copy in swap + spread[0] + spread[1]:
        copy.wait_send()


def products(v_ref, sym_ref, link_ref, o):
    n = v_ref.shape[1]
    p, q = as_right(v_ref[:n]), as_right(v_ref[n:])

    def rows(first, count):
        return v_ref[pl.ds(pl.multiple_of(first, count), count), :]

    for t, right in enumerate((p, q)):
        top = rows(t * n + o * ROWS, ROWS)
        bottom = rows(t * n + (2 * SLOTS - 1 - o) * ROWS, ROWS)
        both = dot_nt(as_left(jnp.concatenate([top, bottom], axis=0)), right)
        sym_ref[t] = pack(both[:ROWS], both[ROWS:], o)
    if link_ref is None:
        return
    part = link_ref.shape[1]
    for t, right in enumerate((q, p)):
        link_ref[t] = -dot_nt(as_left(rows(t * n + o * part, part)), right)


def first_level_kernel(
    coef_ref, s_ref, m_ref, g_ref, own_ref, sym_ref, link_ref,
    mine_ref, got_ref, a_ref, above_ref, z_ref, v_ref, inv_ref, ds, dr, gs, gr,
):
    i, y, c = place()
    chips, other = near()
    o = y * 2 + c
    n = z_ref.shape[0]
    part = above_ref.shape[1]
    down = (along(i, -1), o)
    up = (along(i, 1), o)
    enter(chips + [other, down, up])
    mine = pack_rows(m_ref, o)
    mine_ref[...] = mine
    own = m_ref.at[pl.ds(pl.multiple_of(o * part, part), part)]
    copies = [
        remote(mine_ref, got_ref, ds.at[0], dr.at[0], down),
        remote(own, above_ref.at[o], ds.at[1], dr.at[1], down),
    ]
    for copy in copies:
        copy.start()
    gather = Gather(a_ref, gs.at[0], gr.at[0])
    gather_above = Gather(above_ref, gs.at[1], gr.at[1])
    before, rate0, rate1, up1, rate2 = rates(coef_ref)
    rows = (1.0 + rate1 * rate1) * pack_rows(s_ref, o) + g_ref[...] - (rate0 * rate0) * mine
    copies[0].wait_recv()
    rows = rows - (up1 * up1) * got_ref[...]
    own_ref[...] = rows
    a_ref[o] = rows
    gather.start()
    v_ref[:n] = -(before * rate0) * m_ref[...]
    gather.forward()
    copies[1].wait_recv()
    gather_above.start()
    gather.finish()
    unpack(z_ref, a_ref)

    half = v_ref.at[:n]

    def between(k):
        if k < 2:
            solve_step(half, z_ref, inv_ref, k)
        else:
            solve_step(v_ref, z_ref, inv_ref, k)
        if k == 0:
            gather_above.forward()
        if k == 1:
            gather_above.finish()
            v_ref[n:] = -(up1 * rate2) * above_ref[...].reshape(n, n)
            solve_step(v_ref, z_ref, inv_ref, 0, n)
            solve_step(v_ref, z_ref, inv_ref, 1, n)

    factor(z_ref, inv_ref, between)
    products(v_ref, sym_ref, link_ref, o)
    for copy in copies:
        copy.wait_send()


def level_kernel(
    stride, last, old_ref, sym_ref, link_ref, own_ref, next_sym_ref, *refs
):
    next_link_ref = None if last else refs[0]
    (
    got_ref, a_ref, p_ref, q_ref, z_ref, v_ref, inv_ref, ds, dr, gs, gr,
    ) = refs if last else refs[1:]
    i, y, c = place()
    chips, other = near()
    o = y * 2 + c
    n = z_ref.shape[0]
    down = (along(i, -stride), o)
    up = (along(i, stride), o)
    enter(chips + [other, down, up])
    copies = [
        remote(sym_ref.at[0], got_ref.at[0], ds.at[0], dr.at[0], down),
        remote(sym_ref.at[1], got_ref.at[1], ds.at[1], dr.at[1], up),
        remote(link_ref.at[0], p_ref.at[o], ds.at[2], dr.at[2], up),
        remote(link_ref.at[1], q_ref.at[o], ds.at[3], dr.at[3], down),
    ]
    for copy in copies:
        copy.start()
    gather = Gather(a_ref, gs.at[0], gr.at[0])
    links = [Gather(p_ref, gs.at[1], gr.at[1]), Gather(q_ref, gs.at[2], gr.at[2])]
    copies[0].wait_recv()
    copies[1].wait_recv()
    rows = old_ref[...] - got_ref[0] - got_ref[1]
    own_ref[...] = rows
    a_ref[o] = rows
    gather.start()
    gather.forward()
    for copy, link in zip(copies[2:], links):
        copy.wait_recv()
        link.start()
    gather.finish()
    unpack(z_ref, a_ref)

    def between(k):
        if k == 1:
            for link in links:
                link.forward()
        if k == 2:
            for link in links:
                link.finish()
            v_ref[:n] = p_ref[...].reshape(n, n)
            v_ref[n:] = q_ref[...].reshape(n, n)
            solve_step(v_ref, z_ref, inv_ref, 0)
            solve_step(v_ref, z_ref, inv_ref, 1)
        if k >= 2:
            solve_step(v_ref, z_ref, inv_ref, k)

    factor(z_ref, inv_ref, between)
    products(v_ref, next_sym_ref, next_link_ref, o)
    for copy in copies:
        copy.wait_send()


def final_kernel(
    stride, old_ref, sym_ref, l_ref, got_ref, a_ref, z_ref, inv_ref, ds, dr, gs, gr
):
    i, y, c = place()
    chips, other = near()
    o = y * 2 + c
    n = z_ref.shape[0]
    down = (along(i, -stride), o)
    up = (along(i, stride), o)
    enter(chips + [other, down, up])
    copies = [
        remote(sym_ref.at[0], got_ref.at[0], ds.at[0], dr.at[0], down),
        remote(sym_ref.at[1], got_ref.at[1], ds.at[1], dr.at[1], up),
    ]
    for copy in copies:
        copy.start()
    gather = Gather(a_ref, gs, gr)
    copies[0].wait_recv()
    copies[1].wait_recv()
    a_ref[o] = old_ref[...] - got_ref[0] - got_ref[1]
    gather.start()
    gather.forward()
    gather.finish()
    unpack(z_ref, a_ref)
    factor(z_ref, inv_ref)
    row = lax.broadcasted_iota(jnp.int32, (n, n), 0)
    col = lax.broadcasted_iota(jnp.int32, (n, n), 1)
    l_ref[...] = jnp.where(col <= row, z_ref[...], 0.0)
    for copy in copies:
        copy.wait_send()


VMEM = pl.BlockSpec(memory_space=pltpu.VMEM)
SMEM = pl.BlockSpec(memory_space=pltpu.SMEM)
DMA = pltpu.SemaphoreType.DMA


def f32(*shape):
    return jax.ShapeDtypeStruct(shape, jnp.float32)


def scratch(*shape):
    return pltpu.VMEM(shape, jnp.float32)


def call(kernel, out_shape, in_specs, scratch_shapes=(), collective_id=None):
    extra = {}
    if collective_id is not None:
        extra = dict(collective_id=collective_id, has_side_effects=True)
    return pl.pallas_call(
        kernel,
        out_shape=out_shape,
        in_specs=in_specs,
        out_specs=jax.tree.map(lambda _: VMEM, out_shape),
        scratch_shapes=scratch_shapes,
        compiler_params=pltpu.CompilerParams(vmem_limit_bytes=VMEM_LIMIT, **extra),
    )


def per_device(basis, obs_weight, col_pattern, tile_block, spatial_prec, time_coef):
    segments = lax.axis_size("tm")
    copies = lax.axis_size("obs")
    n = spatial_prec.shape[0]
    part = n // copies
    piece = (ROWS, WIDE)
    hops = 2 * CHIPS - 1

    grams = call(
        scaled_tiles_gram,
        f32(TB_DEV, CHIPS, 2, *piece),
        [VMEM, VMEM, SMEM, SMEM],
    )(basis, obs_weight, col_pattern, tile_block)
    blocks = scratch(n // BLK, BLK, BLK)
    middle, gram1 = call(
        segment_kernel,
        (f32(n, n), f32(*piece)),
        [SMEM, VMEM, VMEM],
        [
            scratch(SLOTS, *piece),
            scratch(TB_DEV, CHIPS, *piece),
            scratch(TB_DEV, CHIPS, *piece),
            scratch(TB_DEV, CHIPS - 1, *piece),
            scratch(n, n),
            scratch(n, n),
            blocks,
            DMA((TB_DEV,)),
            DMA((TB_DEV,)),
            DMA((TB_DEV, CHIPS - 1)),
            DMA((TB_DEV, CHIPS - 1)),
            DMA((hops,)),
            DMA((hops,)),
        ],
        collective_id=1,
    )(time_coef, spatial_prec, grams)

    results = (f32(*piece), f32(2, *piece), f32(2, part, n))
    work = [scratch(n, n), scratch(2 * n, n), blocks]
    slabs = scratch(copies, part, n)
    pieces = scratch(SLOTS, *piece)
    own_piece, sym, link = call(
        first_level_kernel,
        results,
        [SMEM, VMEM, VMEM, VMEM],
        [scratch(*piece), scratch(*piece), pieces, slabs, *work]
        + [DMA((2,)), DMA((2,)), DMA((2, hops)), DMA((2, hops))],
        collective_id=2,
    )(time_coef, spatial_prec, middle, gram1)

    stride = 1
    while 2 * stride < segments:
        last = 4 * stride >= segments
        own_piece, sym, *more = call(
            functools.partial(level_kernel, stride, last),
            results[:2] if last else results,
            [VMEM, VMEM, VMEM],
            [scratch(2, *piece), pieces, slabs, slabs, *work]
            + [DMA((4,)), DMA((4,)), DMA((3, hops)), DMA((3, hops))],
            collective_id=2 + stride,
        )(own_piece, sym, link)
        link = more[0] if more else None
        stride = 2 * stride

    factor_out = call(
        functools.partial(final_kernel, stride),
        f32(n, n),
        [VMEM, VMEM],
        [scratch(2, *piece), pieces, scratch(n, n), blocks]
        + [DMA((2,)), DMA((2,)), DMA((hops,)), DMA((hops,))],
        collective_id=2 + stride,
    )(own_piece, sym)
    return factor_out[None]


def solution(mesh):
    in_specs = (
        P(("tm", "obs"), None, None),
        P(("tm", "obs"), None),
        P(("tm", "obs"), None),
        P(("tm", "obs")),
        P(),
        P(),
    )
    out_specs = P("tm", None, None)
    return jax.shard_map(
        per_device, mesh=mesh, in_specs=in_specs, out_specs=out_specs, check_vma=False
    )
```

```python
import functools

import jax
import jax.numpy as jnp
from jax import lax
from jax.experimental import pallas as pl
from jax.experimental.pallas import tpu as pltpu
from jax.sharding import PartitionSpec as P

CT = 128
TB_DEV = 2
BLK = 128
VMEM_LIMIT = 48 * 1024 * 1024


def sub_bcast(x, k):
    return jnp.broadcast_to(x[k : k + 1, :], (8, BLK))


def lane_bcast(x, c):
    return jnp.broadcast_to(x[:, c : c + 1], (8, BLK))


def inverse_factor(rest):
    lane = lax.broadcasted_iota(jnp.int32, (8, BLK), 1)
    sub = lax.broadcasted_iota(jnp.int32, (8, BLK), 0)
    rows = []
    groups = BLK // 8
    for g in range(groups):
        own = rest[:8]
        cols = [lane_bcast(own, 8 * g + k) for k in range(8)]
        in_panel = (lane >= 8 * g) & (lane < 8 * g + 8)
        eye = (lane - 8 * g == sub).astype(jnp.float32)
        unit = jnp.where(in_panel, eye, own)
        full = unit
        scale = jnp.zeros((8, BLK), jnp.float32)
        for k in range(0, 8, 2):
            b0, b1 = cols[k], cols[k + 1]
            p, q, r = sub_bcast(b0, k), sub_bcast(b0, k + 1), sub_bcast(b1, k + 1)
            det = p * r - q * q
            inv = 1.0 / det
            m0 = (b0 * r - b1 * q) * inv
            m1 = (b1 * p - b0 * q) * inv
            qi = q * inv
            first, second = sub == k, sub == k + 1
            pair = first | second
            f0 = jnp.where(first, -(r * inv), jnp.where(second, qi, m0))
            f1 = jnp.where(first, qi, jnp.where(second, -(p * inv), m1))
            for j in range(k + 2, 8):
                cols[j] = (
                    jnp.where(pair, 0.0, cols[j])
                    - f0 * sub_bcast(cols[j], k)
                    - f1 * sub_bcast(cols[j], k + 1)
                )
            if g < groups - 1:
                full = (
                    jnp.where(pair, 0.0, full)
                    - f0 * sub_bcast(full, k)
                    - f1 * sub_bcast(full, k + 1)
                )
            ip = 1.0 / p
            below = sub > k + 1
            n0 = jnp.where(below, m0, jnp.where(second, q * ip, 0.0))
            n1 = jnp.where(below, m1, 0.0)
            unit = unit - n0 * sub_bcast(unit, k) - n1 * sub_bcast(unit, k + 1)
            scale = jnp.where(
                first, lax.rsqrt(p), jnp.where(second, lax.rsqrt(det * ip), scale)
            )
        rows.append(unit * scale)
        if g < groups - 1:
            rest = rest[8:]
            near, far = rest[:8], rest[8:]
            t = [lane_bcast(near, 8 * g + k) * sub_bcast(full, k) for k in range(8)]
            near = jnp.where(in_panel, 0.0, near) - (
                ((t[0] + t[1]) + (t[2] + t[3])) + ((t[4] + t[5]) + (t[6] + t[7]))
            )
            if g < groups - 2:
                zeros = jnp.zeros((8, BLK), jnp.float32)
                spread = jnp.concatenate(
                    [full if h == g else zeros for h in range(groups)], axis=0
                )
                hi, lo = split(spread)
                wide = lax.broadcasted_iota(jnp.int32, far.shape, 1)
                passed = (wide >= 8 * g) & (wide < 8 * g + 8)
                update = lax.dot_general(
                    as_left(far),
                    jnp.concatenate([hi, hi, lo], axis=0),
                    (((1,), (0,)), ((), ())),
                    preferred_element_type=jnp.float32,
                )
                far = jnp.where(passed, 0.0, far) - update
                rest = jnp.concatenate([near, far], axis=0)
            else:
                rest = near
    return rows


def split(x):
    hi = x.astype(jnp.bfloat16)
    return hi, (x - hi.astype(jnp.float32)).astype(jnp.bfloat16)


def as_left(x):
    hi, lo = split(x)
    return jnp.concatenate([hi, lo, hi], axis=1)


def as_right(x):
    hi, lo = split(x)
    return jnp.concatenate([hi, hi, lo], axis=1)


def dot_nt(left, right):
    return lax.dot_general(
        left, right, (((1,), (1,)), ((), ())), preferred_element_type=jnp.float32
    )


def factor(z_ref, inv_ref, between=None):
    lane = lax.broadcasted_iota(jnp.int32, (8, BLK), 1)
    sub = lax.broadcasted_iota(jnp.int32, (8, BLK), 0)
    steps = z_ref.shape[0] // BLK
    for k in range(steps):
        c = k * BLK
        rows = inverse_factor(z_ref[c : c + BLK, c : c + BLK])
        for g, row in enumerate(rows):
            inv_ref[k, 8 * g : 8 * g + 8, :] = jnp.where(lane <= sub + 8 * g, row, 0.0)
        column = dot_nt(as_left(z_ref[c:, c : c + BLK]), as_right(inv_ref[k]))
        z_ref[c:, c : c + BLK] = column
        if k < steps - 1:
            left, right = as_left(column[BLK:]), as_right(column[BLK:])
            for b in range(c + BLK, z_ref.shape[0], BLK):
                r = b - c - BLK
                z_ref[b:, b : b + BLK] -= dot_nt(left[r:], right[r : r + BLK])
        if between is not None:
            between(k)


def solve_step(v_ref, z_ref, inv_ref, k, first=0):
    c = k * BLK
    column = dot_nt(as_left(v_ref[first:, c : c + BLK]), as_right(inv_ref[k]))
    v_ref[first:, c : c + BLK] = column
    if c + BLK < z_ref.shape[0]:
        v_ref[first:, c + BLK :] -= dot_nt(
            as_left(column), as_right(z_ref[c + BLK :, c : c + BLK])
        )


SLOTS = 8
ROWS = 32
WIDE = 640


def split_at(s):
    return (s // 4 + 1) * BLK


def pack(top, bottom, s):
    def piece(w):
        return jnp.concatenate([top[:, :w], bottom[:, : WIDE - w]], axis=1)

    return jnp.where(s < 4, piece(BLK), piece(2 * BLK))


def pack_rows(ref, s):
    top = ref[pl.ds(pl.multiple_of(s * ROWS, ROWS), ROWS), :]
    bottom = ref[pl.ds(pl.multiple_of((2 * SLOTS - 1 - s) * ROWS, ROWS), ROWS), :]
    return pack(top, bottom, s)


HALVES = 2
HALF = ROWS // HALVES


def half_rows(h):
    return slice(h * HALF, (h + 1) * HALF)


def unpack(z_ref, packed_ref):
    for h in range(HALVES):
        for s in range(SLOTS):
            w = split_at(s)
            top = s * ROWS + h * HALF
            bottom = (2 * SLOTS - 1 - s) * ROWS + h * HALF
            z_ref[top : top + HALF, :w] = packed_ref[h, s, :, :w]
            z_ref[bottom : bottom + HALF, : WIDE - w] = packed_ref[h, s, :, w:]


def scaled_tiles_gram(basis_ref, weight_ref, pattern_ref, block_ref, out_ref):
    tiles, _, columns = basis_ref.shape
    root = jnp.sqrt(weight_ref[...]).T
    lane = lax.broadcasted_iota(jnp.int32, (1, columns), 1) // CT
    out_ref[...] = jnp.zeros_like(out_ref)
    for t in range(tiles):
        mask = jnp.zeros((1, columns), jnp.float32)
        for j in range(columns // CT):
            mask = jnp.where(lane == j, pattern_ref[t, j].astype(jnp.float32), mask)
        raw = basis_ref[t].astype(jnp.float32) * mask
        x = (root[:, t : t + 1] * raw).astype(jnp.bfloat16)
        gram = lax.dot_general(
            x, x, (((0,), (0,)), ((), ())), preferred_element_type=jnp.float32
        )
        m = lax.rem(block_ref[t], TB_DEV)
        for s in range(SLOTS):
            w = split_at(s)
            r = (2 * SLOTS - 1 - s) * ROWS
            out_ref[m, s // 2, s % 2, :, :w] += gram[s * ROWS : (s + 1) * ROWS, :w]
            out_ref[m, s // 2, s % 2, :, w:] += gram[r : r + ROWS, : WIDE - w]


def place():
    where = lax.axis_index("obs")
    return lax.axis_index("tm"), where // 2, lax.rem(where, 2)


def enter(devices):
    barrier = pltpu.get_barrier_semaphore()
    for device in devices:
        pl.semaphore_signal(
            barrier, inc=1, device_id=device, device_id_type=pl.DeviceIdType.MESH
        )
    pl.semaphore_wait(barrier, len(devices))


def remote(src, dst, send, recv, device):
    return pltpu.make_async_remote_copy(
        src_ref=src,
        dst_ref=dst,
        send_sem=send,
        recv_sem=recv,
        device_id=device,
        device_id_type=pl.DeviceIdType.MESH,
    )


CHIPS = 4


def near():
    i, y, c = place()
    chips = [(i, lax.rem(y + d, CHIPS) * 2 + c) for d in range(1, CHIPS)]
    return chips, (i, y * 2 + 1 - c)


class Gather:
    def __init__(self, ref, send, recv):
        _, y, c = place()
        chips, other = near()
        own = ref.at[y * 2 + c]
        self.out = [
            remote(own, own, send.at[d], recv.at[d], chips[d]) for d in range(CHIPS - 1)
        ]
        self.cross, self.back = [], []
        for d in range(CHIPS):
            from_chip = lax.rem(y + CHIPS - d, CHIPS) * 2
            mine, theirs = ref.at[from_chip + c], ref.at[from_chip + 1 - c]
            sems = send.at[CHIPS - 1 + d], recv.at[CHIPS - 1 + d]
            self.cross.append(remote(mine, mine, *sems, other))
            self.back.append(remote(theirs, theirs, *sems, other))
        self.arrive = [
            remote(
                ref.at[lax.rem(y + CHIPS - d, CHIPS) * 2 + c],
                ref.at[lax.rem(y + CHIPS - d, CHIPS) * 2 + c],
                send.at[d - 1],
                recv.at[d - 1],
                chips[d - 1],
            )
            for d in range(1, CHIPS)
        ]

    def start(self):
        for copy in self.out:
            copy.start()
        self.cross[0].start()

    def forward(self):
        for d in (1, 3, 2):
            self.arrive[d - 1].wait_recv()
            self.cross[d].start()

    def finish(self):
        for copy in self.out + self.cross:
            copy.wait_send()
        for copy in self.back:
            copy.wait_recv()


def share(ref, send, recv):
    return [Gather(ref.at[h], send.at[h], recv.at[h]) for h in range(HALVES)]


def finish(gathers):
    for gather in gathers:
        gather.forward()
    for gather in gathers:
        gather.finish()


def rates(coef_ref):
    i, _, _ = place()
    count, last = coef_ref.shape[0], lax.axis_size("tm") - 1
    first = i * TB_DEV
    before = jnp.where(i > 0, coef_ref[lax.rem(first + count - 1, count)], 0.0)
    rate0, rate1 = coef_ref[first], coef_ref[first + 1]
    return before, rate0, rate1, jnp.where(i < last, rate1, 0.0), coef_ref[lax.rem(first + 2, count)]


def along(i, distance):
    count = lax.axis_size("tm")
    return lax.rem(i + count + distance, count)


def segment_kernel(
    coef_ref, s_ref, part_ref, m_ref, second_ref,
    first_ref, other_ref, sum_ref, got_ref, z_ref, v_ref, inv_ref, xs, xr, ss, sr, gs, gr,
):
    i, y, c = place()
    chips, other = near()
    enter(chips + [other])
    parts = [(0, half_rows(0)), (0, half_rows(1)), (1, slice(0, ROWS))]
    swap = [
        remote(part_ref.at[t, :, 1 - c, r], other_ref.at[t, :, r], xs.at[j], xr.at[j], other)
        for j, (t, r) in enumerate(parts)
    ]
    spread = [
        [
            remote(
                sum_ref.at[t, lax.rem(y + d, CHIPS), r],
                got_ref.at[t, d - 1, r],
                ss.at[j, d - 1],
                sr.at[j, d - 1],
                chips[d - 1],
            )
            for d in range(1, CHIPS)
        ]
        for j, (t, r) in enumerate(parts)
    ]
    gathers = share(first_ref, gs, gr)

    def chip_sum(j):
        t, r = parts[j]
        swap[j].wait_recv()
        sum_ref[t, :, r] = part_ref[t, :, c, r] + other_ref[t, :, r]

    def total(j):
        t, r = parts[j]
        for copy in spread[j]:
            copy.wait_recv()
        return (sum_ref[t, y, r] + got_ref[t, 0, r]) + (got_ref[t, 1, r] + got_ref[t, 2, r])

    for copy in swap:
        copy.start()
    for h in range(HALVES):
        chip_sum(h)
        for copy in spread[h]:
            copy.start()
    v_ref[...] = s_ref[...]
    for h in range(HALVES):
        first_ref[h, y * 2 + c] = total(h)
        gathers[h].start()
    chip_sum(2)
    finish(gathers)
    for copy in spread[2]:
        copy.start()
    unpack(z_ref, first_ref)
    _, rate0, _, _, _ = rates(coef_ref)
    z_ref[...] += (1.0 + rate0 * rate0) * s_ref[...]

    def between(k):
        if k == 2:
            second_ref[...] = total(2)
        solve_step(v_ref, z_ref, inv_ref, k)

    factor(z_ref, inv_ref, between)
    solved = v_ref[...]
    m_ref[...] = dot_nt(as_left(solved), as_right(solved))
    for copy in swap + spread[0] + spread[1] + spread[2]:
        copy.wait_send()


def products(v_ref, sym_ref, link_ref, o):
    n = v_ref.shape[1]
    p, q = as_right(v_ref[:n]), as_right(v_ref[n:])

    def rows(first, count):
        return v_ref[pl.ds(pl.multiple_of(first, count), count), :]

    for t, right in enumerate((p, q)):
        top = rows(t * n + o * ROWS, ROWS)
        bottom = rows(t * n + (2 * SLOTS - 1 - o) * ROWS, ROWS)
        both = dot_nt(as_left(jnp.concatenate([top, bottom], axis=0)), right)
        sym_ref[t] = pack(both[:ROWS], both[ROWS:], o)
    if link_ref is None:
        return
    part = link_ref.shape[1]
    for t, right in enumerate((q, p)):
        link_ref[t] = -dot_nt(as_left(rows(t * n + o * part, part)), right)


def first_level_kernel(
    coef_ref, s_ref, m_ref, g_ref, own_ref, sym_ref, link_ref,
    mine_ref, got_ref, a_ref, above_ref, z_ref, v_ref, inv_ref, ds, dr, gs, gr,
):
    i, y, c = place()
    chips, other = near()
    o = y * 2 + c
    n = z_ref.shape[0]
    part = above_ref.shape[1]
    down = (along(i, -1), o)
    up = (along(i, 1), o)
    enter(chips + [other, down, up])
    mine = pack_rows(m_ref, o)
    mine_ref[...] = mine
    own = m_ref.at[pl.ds(pl.multiple_of(o * part, part), part)]
    pieces = [
        remote(mine_ref.at[half_rows(h)], got_ref.at[half_rows(h)], ds.at[h], dr.at[h], down)
        for h in range(HALVES)
    ]
    whole = remote(own, above_ref.at[o], ds.at[HALVES], dr.at[HALVES], down)
    for copy in pieces:
        copy.start()
    gathers = share(a_ref, gs, gr)
    gather_above = Gather(above_ref, gs.at[HALVES], gr.at[HALVES])
    before, rate0, rate1, up1, rate2 = rates(coef_ref)
    rows = (1.0 + rate1 * rate1) * pack_rows(s_ref, o) + g_ref[...] - (rate0 * rate0) * mine
    own_ref[...] = rows
    for h in range(HALVES):
        r = half_rows(h)
        pieces[h].wait_recv()
        part_rows = own_ref[r] - (up1 * up1) * got_ref[r]
        own_ref[r] = part_rows
        a_ref[h, o] = part_rows
        gathers[h].start()
    whole.start()
    v_ref[:n] = -(before * rate0) * m_ref[...]
    finish(gathers)
    unpack(z_ref, a_ref)
    whole.wait_recv()
    gather_above.start()
    half = v_ref.at[:n]

    def between(k):
        if k < 3:
            solve_step(half, z_ref, inv_ref, k)
        else:
            solve_step(v_ref, z_ref, inv_ref, k)
        if k == 1:
            gather_above.forward()
        if k == 2:
            gather_above.finish()
            v_ref[n:] = -(up1 * rate2) * above_ref[...].reshape(n, n)
            for step in range(3):
                solve_step(v_ref, z_ref, inv_ref, step, n)

    factor(z_ref, inv_ref, between)
    products(v_ref, sym_ref, link_ref, o)
    for copy in pieces + [whole]:
        copy.wait_send()


def corrections(old_ref, sym_ref, got_ref, a_ref, own_ref, down, up, o, ds, dr, gs, gr):
    copies = [
        [
            remote(
                sym_ref.at[t, half_rows(h)],
                got_ref.at[t, half_rows(h)],
                ds.at[2 * h + t],
                dr.at[2 * h + t],
                device,
            )
            for t, device in enumerate((down, up))
        ]
        for h in range(HALVES)
    ]
    for pair in copies:
        for copy in pair:
            copy.start()
    gathers = share(a_ref, gs, gr)
    for h, pair in enumerate(copies):
        r = half_rows(h)
        for copy in pair:
            copy.wait_recv()
        rows = old_ref[r] - got_ref[0, r] - got_ref[1, r]
        if own_ref is not None:
            own_ref[r] = rows
        a_ref[h, o] = rows
        gathers[h].start()
    return copies[0] + copies[1], gathers


def level_kernel(
    stride, last, old_ref, sym_ref, link_ref, own_ref, next_sym_ref, *refs
):
    next_link_ref = None if last else refs[0]
    (
    got_ref, a_ref, p_ref, q_ref, z_ref, v_ref, inv_ref, ds, dr, gs, gr,
    ) = refs if last else refs[1:]
    i, y, c = place()
    chips, other = near()
    o = y * 2 + c
    n = z_ref.shape[0]
    down = (along(i, -stride), o)
    up = (along(i, stride), o)
    enter(chips + [other, down, up])
    copies, gathers = corrections(
        old_ref, sym_ref, got_ref, a_ref, own_ref, down, up, o, ds, dr, gs, gr
    )
    moved = [
        remote(link_ref.at[0], p_ref.at[o], ds.at[4], dr.at[4], up),
        remote(link_ref.at[1], q_ref.at[o], ds.at[5], dr.at[5], down),
    ]
    for copy in moved:
        copy.start()
    p_link = Gather(p_ref, gs.at[HALVES], gr.at[HALVES])
    q_link = Gather(q_ref, gs.at[HALVES + 1], gr.at[HALVES + 1])
    finish(gathers)
    unpack(z_ref, a_ref)

    def begin_links():
        for copy, link in zip(moved, (p_link, q_link)):
            copy.wait_recv()
            link.start()

    late = stride == 2
    if not late:
        begin_links()
    half = v_ref.at[:n]

    def between(k):
        if k == 0 and late:
            begin_links()
        if k == 1 and not late:
            p_link.forward()
        if k == 2:
            if late:
                p_link.forward()
            p_link.finish()
            v_ref[:n] = p_ref[...].reshape(n, n)
            for step in range(3):
                solve_step(half, z_ref, inv_ref, step)
            if not late:
                q_link.forward()
        if k == 3:
            if late:
                q_link.forward()
            q_link.finish()
            v_ref[n:] = q_ref[...].reshape(n, n)
            for step in range(3):
                solve_step(v_ref, z_ref, inv_ref, step, n)
            solve_step(v_ref, z_ref, inv_ref, 3)

    factor(z_ref, inv_ref, between)
    products(v_ref, next_sym_ref, next_link_ref, o)
    for copy in copies + moved:
        copy.wait_send()


def final_kernel(
    stride, old_ref, sym_ref, l_ref, got_ref, a_ref, z_ref, inv_ref, ds, dr, gs, gr
):
    i, y, c = place()
    chips, other = near()
    o = y * 2 + c
    n = z_ref.shape[0]
    down = (along(i, -stride), o)
    up = (along(i, stride), o)
    enter(chips + [other, down, up])
    copies, gathers = corrections(
        old_ref, sym_ref, got_ref, a_ref, None, down, up, o, ds, dr, gs, gr
    )
    finish(gathers)
    unpack(z_ref, a_ref)
    factor(z_ref, inv_ref)
    row = lax.broadcasted_iota(jnp.int32, (n, n), 0)
    col = lax.broadcasted_iota(jnp.int32, (n, n), 1)
    l_ref[...] = jnp.where(col <= row, z_ref[...], 0.0)
    for copy in copies:
        copy.wait_send()


VMEM = pl.BlockSpec(memory_space=pltpu.VMEM)
SMEM = pl.BlockSpec(memory_space=pltpu.SMEM)
DMA = pltpu.SemaphoreType.DMA


def f32(*shape):
    return jax.ShapeDtypeStruct(shape, jnp.float32)


def scratch(*shape):
    return pltpu.VMEM(shape, jnp.float32)


def call(kernel, out_shape, in_specs, scratch_shapes=(), collective_id=None):
    extra = {}
    if collective_id is not None:
        extra = dict(collective_id=collective_id, has_side_effects=True)
    return pl.pallas_call(
        kernel,
        out_shape=out_shape,
        in_specs=in_specs,
        out_specs=jax.tree.map(lambda _: VMEM, out_shape),
        scratch_shapes=scratch_shapes,
        compiler_params=pltpu.CompilerParams(vmem_limit_bytes=VMEM_LIMIT, **extra),
    )


def per_device(basis, obs_weight, col_pattern, tile_block, spatial_prec, time_coef):
    segments = lax.axis_size("tm")
    copies = lax.axis_size("obs")
    n = spatial_prec.shape[0]
    part = n // copies
    piece = (ROWS, WIDE)
    hops = 2 * CHIPS - 1

    grams = call(
        scaled_tiles_gram,
        f32(TB_DEV, CHIPS, 2, *piece),
        [VMEM, VMEM, SMEM, SMEM],
    )(basis, obs_weight, col_pattern, tile_block)
    blocks = scratch(n // BLK, BLK, BLK)
    pieces = scratch(HALVES, SLOTS, HALF, WIDE)
    middle, gram1 = call(
        segment_kernel,
        (f32(n, n), f32(*piece)),
        [SMEM, VMEM, VMEM],
        [
            pieces,
            scratch(TB_DEV, CHIPS, *piece),
            scratch(TB_DEV, CHIPS, *piece),
            scratch(TB_DEV, CHIPS - 1, *piece),
            scratch(n, n),
            scratch(n, n),
            blocks,
            DMA((HALVES + 1,)),
            DMA((HALVES + 1,)),
            DMA((HALVES + 1, CHIPS - 1)),
            DMA((HALVES + 1, CHIPS - 1)),
            DMA((HALVES, hops)),
            DMA((HALVES, hops)),
        ],
        collective_id=1,
    )(time_coef, spatial_prec, grams)

    results = (f32(*piece), f32(2, *piece), f32(2, part, n))
    work = [scratch(n, n), scratch(2 * n, n), blocks]
    slabs = scratch(copies, part, n)
    own_piece, sym, link = call(
        first_level_kernel,
        results,
        [SMEM, VMEM, VMEM, VMEM],
        [scratch(*piece), scratch(*piece), pieces, slabs, *work]
        + [DMA((HALVES + 1,)), DMA((HALVES + 1,))]
        + [DMA((HALVES + 1, hops)), DMA((HALVES + 1, hops))],
        collective_id=2,
    )(time_coef, spatial_prec, middle, gram1)

    stride = 1
    while 2 * stride < segments:
        last = 4 * stride >= segments
        own_piece, sym, *more = call(
            functools.partial(level_kernel, stride, last),
            results[:2] if last else results,
            [VMEM, VMEM, VMEM],
            [scratch(2, *piece), pieces, slabs, slabs, *work]
            + [DMA((6,)), DMA((6,)), DMA((HALVES + 2, hops)), DMA((HALVES + 2, hops))],
            collective_id=2 + stride,
        )(own_piece, sym, link)
        link = more[0] if more else None
        stride = 2 * stride

    factor_out = call(
        functools.partial(final_kernel, stride),
        f32(n, n),
        [VMEM, VMEM],
        [scratch(2, *piece), pieces, scratch(n, n), blocks]
        + [DMA((4,)), DMA((4,)), DMA((HALVES, hops)), DMA((HALVES, hops))],
        collective_id=2 + stride,
    )(own_piece, sym)
    return factor_out[None]


def solution(mesh):
    in_specs = (
        P(("tm", "obs"), None, None),
        P(("tm", "obs"), None),
        P(("tm", "obs"), None),
        P(("tm", "obs")),
        P(),
        P(),
    )
    out_specs = P("tm", None, None)
    return jax.shard_map(
        per_device, mesh=mesh, in_specs=in_specs, out_specs=out_specs, check_vma=False
    )
```

```python
import functools

import jax
import jax.numpy as jnp
from jax import lax
from jax.experimental import pallas as pl
from jax.experimental.pallas import tpu as pltpu
from jax.sharding import PartitionSpec as P

CT = 128
TB_DEV = 2
BLK = 128
VMEM_LIMIT = 48 * 1024 * 1024


def sub_bcast(x, k):
    return jnp.broadcast_to(x[k : k + 1, :], (8, BLK))


def lane_bcast(x, c):
    return jnp.broadcast_to(x[:, c : c + 1], (8, BLK))


def inverse_factor(rest):
    lane = lax.broadcasted_iota(jnp.int32, (8, BLK), 1)
    sub = lax.broadcasted_iota(jnp.int32, (8, BLK), 0)
    rows = []
    groups = BLK // 8
    for g in range(groups):
        own = rest[:8]
        cols = [lane_bcast(own, 8 * g + k) for k in range(8)]
        in_panel = (lane >= 8 * g) & (lane < 8 * g + 8)
        eye = (lane - 8 * g == sub).astype(jnp.float32)
        unit = jnp.where(in_panel, eye, own)
        full = unit
        scale = jnp.zeros((8, BLK), jnp.float32)
        for k in range(0, 8, 2):
            b0, b1 = cols[k], cols[k + 1]
            p, q, r = sub_bcast(b0, k), sub_bcast(b0, k + 1), sub_bcast(b1, k + 1)
            det = p * r - q * q
            inv = 1.0 / det
            m0 = (b0 * r - b1 * q) * inv
            m1 = (b1 * p - b0 * q) * inv
            qi = q * inv
            first, second = sub == k, sub == k + 1
            pair = first | second
            f0 = jnp.where(first, -(r * inv), jnp.where(second, qi, m0))
            f1 = jnp.where(first, qi, jnp.where(second, -(p * inv), m1))
            for j in range(k + 2, 8):
                cols[j] = (
                    jnp.where(pair, 0.0, cols[j])
                    - f0 * sub_bcast(cols[j], k)
                    - f1 * sub_bcast(cols[j], k + 1)
                )
            if g < groups - 1:
                full = (
                    jnp.where(pair, 0.0, full)
                    - f0 * sub_bcast(full, k)
                    - f1 * sub_bcast(full, k + 1)
                )
            ip = 1.0 / p
            below = sub > k + 1
            n0 = jnp.where(below, m0, jnp.where(second, q * ip, 0.0))
            n1 = jnp.where(below, m1, 0.0)
            unit = unit - n0 * sub_bcast(unit, k) - n1 * sub_bcast(unit, k + 1)
            scale = jnp.where(
                first, lax.rsqrt(p), jnp.where(second, lax.rsqrt(det * ip), scale)
            )
        rows.append(unit * scale)
        if g < groups - 1:
            rest = rest[8:]
            near, far = rest[:8], rest[8:]
            t = [lane_bcast(near, 8 * g + k) * sub_bcast(full, k) for k in range(8)]
            near = jnp.where(in_panel, 0.0, near) - (
                ((t[0] + t[1]) + (t[2] + t[3])) + ((t[4] + t[5]) + (t[6] + t[7]))
            )
            if g < groups - 2:
                zeros = jnp.zeros((8, BLK), jnp.float32)
                spread = jnp.concatenate(
                    [full if h == g else zeros for h in range(groups)], axis=0
                )
                hi, lo = split(spread)
                wide = lax.broadcasted_iota(jnp.int32, far.shape, 1)
                passed = (wide >= 8 * g) & (wide < 8 * g + 8)
                update = lax.dot_general(
                    as_left(far),
                    jnp.concatenate([hi, hi, lo], axis=0),
                    (((1,), (0,)), ((), ())),
                    preferred_element_type=jnp.float32,
                )
                far = jnp.where(passed, 0.0, far) - update
                rest = jnp.concatenate([near, far], axis=0)
            else:
                rest = near
    return rows


def split(x):
    hi = x.astype(jnp.bfloat16)
    return hi, (x - hi.astype(jnp.float32)).astype(jnp.bfloat16)


def as_left(x):
    hi, lo = split(x)
    return jnp.concatenate([hi, lo, hi], axis=1)


def as_right(x):
    hi, lo = split(x)
    return jnp.concatenate([hi, hi, lo], axis=1)


def dot_nt(left, right):
    return lax.dot_general(
        left, right, (((1,), (1,)), ((), ())), preferred_element_type=jnp.float32
    )


def factor(z_ref, inv_ref, between=None):
    lane = lax.broadcasted_iota(jnp.int32, (8, BLK), 1)
    sub = lax.broadcasted_iota(jnp.int32, (8, BLK), 0)
    steps = z_ref.shape[0] // BLK
    for k in range(steps):
        c = k * BLK
        rows = inverse_factor(z_ref[c : c + BLK, c : c + BLK])
        for g, row in enumerate(rows):
            inv_ref[k, 8 * g : 8 * g + 8, :] = jnp.where(lane <= sub + 8 * g, row, 0.0)
        column = dot_nt(as_left(z_ref[c:, c : c + BLK]), as_right(inv_ref[k]))
        z_ref[c:, c : c + BLK] = column
        if k < steps - 1:
            left, right = as_left(column[BLK:]), as_right(column[BLK:])
            for b in range(c + BLK, z_ref.shape[0], BLK):
                r = b - c - BLK
                z_ref[b:, b : b + BLK] -= dot_nt(left[r:], right[r : r + BLK])
        if between is not None:
            between(k)


def solve_step(v_ref, z_ref, inv_ref, k, first=0):
    c = k * BLK
    column = dot_nt(as_left(v_ref[first:, c : c + BLK]), as_right(inv_ref[k]))
    v_ref[first:, c : c + BLK] = column
    if c + BLK < z_ref.shape[0]:
        v_ref[first:, c + BLK :] -= dot_nt(
            as_left(column), as_right(z_ref[c + BLK :, c : c + BLK])
        )


SLOTS = 8
ROWS = 32
WIDE = 640


def split_at(s):
    return (s // 4 + 1) * BLK


def pack(top, bottom, s):
    def piece(w):
        return jnp.concatenate([top[:, :w], bottom[:, : WIDE - w]], axis=1)

    return jnp.where(s < 4, piece(BLK), piece(2 * BLK))


def pack_rows(ref, s):
    top = ref[pl.ds(pl.multiple_of(s * ROWS, ROWS), ROWS), :]
    bottom = ref[pl.ds(pl.multiple_of((2 * SLOTS - 1 - s) * ROWS, ROWS), ROWS), :]
    return pack(top, bottom, s)


HALVES = 2
HALF = ROWS // HALVES


def half_rows(h):
    return slice(h * HALF, (h + 1) * HALF)


def collect(z_ref, packed_ref, gathers):
    for gather in gathers:
        gather.forward()
    for h in range(HALVES):
        gathers[h].finish()
        for s in range(SLOTS):
            w = split_at(s)
            top = s * ROWS + h * HALF
            bottom = (2 * SLOTS - 1 - s) * ROWS + h * HALF
            z_ref[top : top + HALF, :w] = packed_ref[h, s, :, :w]
            z_ref[bottom : bottom + HALF, : WIDE - w] = packed_ref[h, s, :, w:]


def scaled_tiles_gram(basis_ref, weight_ref, pattern_ref, block_ref, out_ref):
    tiles, _, columns = basis_ref.shape
    root = jnp.sqrt(weight_ref[...]).T
    lane = lax.broadcasted_iota(jnp.int32, (1, columns), 1) // CT
    out_ref[...] = jnp.zeros_like(out_ref)
    for t in range(tiles):
        mask = jnp.zeros((1, columns), jnp.float32)
        for j in range(columns // CT):
            mask = jnp.where(lane == j, pattern_ref[t, j].astype(jnp.float32), mask)
        raw = basis_ref[t].astype(jnp.float32) * mask
        x = (root[:, t : t + 1] * raw).astype(jnp.bfloat16)
        gram = lax.dot_general(
            x, x, (((0,), (0,)), ((), ())), preferred_element_type=jnp.float32
        )
        m = lax.rem(block_ref[t], TB_DEV)
        for s in range(SLOTS):
            w = split_at(s)
            r = (2 * SLOTS - 1 - s) * ROWS
            out_ref[m, s // 2, s % 2, :, :w] += gram[s * ROWS : (s + 1) * ROWS, :w]
            out_ref[m, s // 2, s % 2, :, w:] += gram[r : r + ROWS, : WIDE - w]


def place():
    where = lax.axis_index("obs")
    return lax.axis_index("tm"), where // 2, lax.rem(where, 2)


def enter(devices):
    barrier = pltpu.get_barrier_semaphore()
    for device in devices:
        pl.semaphore_signal(
            barrier, inc=1, device_id=device, device_id_type=pl.DeviceIdType.MESH
        )
    pl.semaphore_wait(barrier, len(devices))


def remote(src, dst, send, recv, device):
    return pltpu.make_async_remote_copy(
        src_ref=src,
        dst_ref=dst,
        send_sem=send,
        recv_sem=recv,
        device_id=device,
        device_id_type=pl.DeviceIdType.MESH,
    )


CHIPS = 4


def near():
    i, y, c = place()
    chips = [(i, lax.rem(y + d, CHIPS) * 2 + c) for d in range(1, CHIPS)]
    return chips, (i, y * 2 + 1 - c)


class Gather:
    def __init__(self, ref, send, recv):
        _, y, c = place()
        chips, other = near()
        own = ref.at[y * 2 + c]
        self.out = [
            remote(own, own, send.at[d], recv.at[d], chips[d]) for d in range(CHIPS - 1)
        ]
        self.cross, self.back = [], []
        for d in range(CHIPS):
            from_chip = lax.rem(y + CHIPS - d, CHIPS) * 2
            mine, theirs = ref.at[from_chip + c], ref.at[from_chip + 1 - c]
            sems = send.at[CHIPS - 1 + d], recv.at[CHIPS - 1 + d]
            self.cross.append(remote(mine, mine, *sems, other))
            self.back.append(remote(theirs, theirs, *sems, other))
        self.arrive = [
            remote(
                ref.at[lax.rem(y + CHIPS - d, CHIPS) * 2 + c],
                ref.at[lax.rem(y + CHIPS - d, CHIPS) * 2 + c],
                send.at[d - 1],
                recv.at[d - 1],
                chips[d - 1],
            )
            for d in range(1, CHIPS)
        ]

    def start(self):
        for copy in self.out:
            copy.start()
        self.cross[0].start()

    def forward(self):
        for d in (1, 3, 2):
            self.arrive[d - 1].wait_recv()
            self.cross[d].start()

    def finish(self):
        for copy in self.back:
            copy.wait_recv()

    def close(self):
        for copy in self.out + self.cross:
            copy.wait_send()


def share(ref, send, recv):
    return [Gather(ref.at[h], send.at[h], recv.at[h]) for h in range(HALVES)]


def rates(coef_ref):
    i, _, _ = place()
    count, last = coef_ref.shape[0], lax.axis_size("tm") - 1
    first = i * TB_DEV
    before = jnp.where(i > 0, coef_ref[lax.rem(first + count - 1, count)], 0.0)
    rate0, rate1 = coef_ref[first], coef_ref[first + 1]
    return before, rate0, rate1, jnp.where(i < last, rate1, 0.0), coef_ref[lax.rem(first + 2, count)]


def along(i, distance):
    count = lax.axis_size("tm")
    return lax.rem(i + count + distance, count)


def segment_kernel(
    coef_ref, s_ref, part_ref, m_ref, second_ref,
    first_ref, other_ref, sum_ref, got_ref, z_ref, v_ref, inv_ref, xs, xr, ss, sr, gs, gr,
):
    i, y, c = place()
    chips, other = near()
    enter(chips + [other])
    parts = [(0, half_rows(0)), (0, half_rows(1)), (1, slice(0, ROWS))]
    swap = [
        remote(part_ref.at[t, :, 1 - c, r], other_ref.at[t, :, r], xs.at[j], xr.at[j], other)
        for j, (t, r) in enumerate(parts)
    ]
    spread = [
        [
            remote(
                sum_ref.at[t, lax.rem(y + d, CHIPS), r],
                got_ref.at[t, d - 1, r],
                ss.at[j, d - 1],
                sr.at[j, d - 1],
                chips[d - 1],
            )
            for d in range(1, CHIPS)
        ]
        for j, (t, r) in enumerate(parts)
    ]
    gathers = share(first_ref, gs, gr)

    def chip_sum(j):
        t, r = parts[j]
        swap[j].wait_recv()
        sum_ref[t, :, r] = part_ref[t, :, c, r] + other_ref[t, :, r]

    def total(j):
        t, r = parts[j]
        for copy in spread[j]:
            copy.wait_recv()
        return (sum_ref[t, y, r] + got_ref[t, 0, r]) + (got_ref[t, 1, r] + got_ref[t, 2, r])

    for copy in swap:
        copy.start()
    for h in range(HALVES):
        chip_sum(h)
        for copy in spread[h]:
            copy.start()
    v_ref[...] = s_ref[...]
    for h in range(HALVES):
        first_ref[h, y * 2 + c] = total(h)
        gathers[h].start()
    chip_sum(2)
    collect(z_ref, first_ref, gathers)
    for copy in spread[2]:
        copy.start()
    _, rate0, _, _, _ = rates(coef_ref)
    z_ref[...] += (1.0 + rate0 * rate0) * s_ref[...]

    def between(k):
        if k == 2:
            second_ref[...] = total(2)
        solve_step(v_ref, z_ref, inv_ref, k)

    factor(z_ref, inv_ref, between)
    solved = v_ref[...]
    m_ref[...] = dot_nt(as_left(solved), as_right(solved))
    for copy in swap + spread[0] + spread[1] + spread[2]:
        copy.wait_send()
    for gather in gathers:
        gather.close()


def products(v_ref, sym_ref, link_ref, o):
    n = v_ref.shape[1]
    p, q = as_right(v_ref[:n]), as_right(v_ref[n:])

    def rows(first, count):
        return v_ref[pl.ds(pl.multiple_of(first, count), count), :]

    for t, right in enumerate((p, q)):
        left = [
            rows(t * n + o * ROWS, ROWS),
            rows(t * n + (2 * SLOTS - 1 - o) * ROWS, ROWS),
        ]
        if link_ref is not None:
            part = link_ref.shape[1]
            left.append(rows((1 - t) * n + o * part, part))
        both = dot_nt(as_left(jnp.concatenate(left, axis=0)), right)
        sym_ref[t] = pack(both[:ROWS], both[ROWS : 2 * ROWS], o)
        if link_ref is not None:
            link_ref[1 - t] = -both[2 * ROWS :]


def first_level_kernel(
    coef_ref, s_ref, m_ref, g_ref, own_ref, sym_ref, link_ref,
    mine_ref, got_ref, a_ref, above_ref, z_ref, v_ref, inv_ref, ds, dr, gs, gr,
):
    i, y, c = place()
    chips, other = near()
    o = y * 2 + c
    n = z_ref.shape[0]
    part = above_ref.shape[1]
    down = (along(i, -1), o)
    up = (along(i, 1), o)
    enter(chips + [other, down, up])
    mine = pack_rows(m_ref, o)
    mine_ref[...] = mine
    own = m_ref.at[pl.ds(pl.multiple_of(o * part, part), part)]
    pieces = [
        remote(mine_ref.at[half_rows(h)], got_ref.at[half_rows(h)], ds.at[h], dr.at[h], down)
        for h in range(HALVES)
    ]
    whole = remote(own, above_ref.at[o], ds.at[HALVES], dr.at[HALVES], down)
    for copy in pieces:
        copy.start()
    gathers = share(a_ref, gs, gr)
    gather_above = Gather(above_ref, gs.at[HALVES], gr.at[HALVES])
    before, rate0, rate1, up1, rate2 = rates(coef_ref)
    rows = (1.0 + rate1 * rate1) * pack_rows(s_ref, o) + g_ref[...] - (rate0 * rate0) * mine
    own_ref[...] = rows
    for h in range(HALVES):
        r = half_rows(h)
        pieces[h].wait_recv()
        part_rows = own_ref[r] - (up1 * up1) * got_ref[r]
        own_ref[r] = part_rows
        a_ref[h, o] = part_rows
        gathers[h].start()
    whole.start()
    v_ref[:n] = -(before * rate0) * m_ref[...]
    collect(z_ref, a_ref, gathers)
    whole.wait_recv()
    gather_above.start()
    half = v_ref.at[:n]

    def between(k):
        if k < 3:
            solve_step(half, z_ref, inv_ref, k)
        else:
            solve_step(v_ref, z_ref, inv_ref, k)
        if k == 1:
            gather_above.forward()
        if k == 2:
            gather_above.finish()
            v_ref[n:] = -(up1 * rate2) * above_ref[...].reshape(n, n)
            for step in range(3):
                solve_step(v_ref, z_ref, inv_ref, step, n)

    factor(z_ref, inv_ref, between)
    products(v_ref, sym_ref, link_ref, o)
    for copy in pieces + [whole]:
        copy.wait_send()
    for gather in gathers + [gather_above]:
        gather.close()


def corrections(old_ref, sym_ref, got_ref, a_ref, own_ref, down, up, o, ds, dr, gs, gr):
    copies = [
        [
            remote(
                sym_ref.at[t, half_rows(h)],
                got_ref.at[t, half_rows(h)],
                ds.at[2 * h + t],
                dr.at[2 * h + t],
                device,
            )
            for t, device in enumerate((down, up))
        ]
        for h in range(HALVES)
    ]
    for pair in copies:
        for copy in pair:
            copy.start()
    gathers = share(a_ref, gs, gr)
    for h, pair in enumerate(copies):
        r = half_rows(h)
        for copy in pair:
            copy.wait_recv()
        rows = old_ref[r] - got_ref[0, r] - got_ref[1, r]
        if own_ref is not None:
            own_ref[r] = rows
        a_ref[h, o] = rows
        gathers[h].start()
    return copies[0] + copies[1], gathers


def level_kernel(
    stride, last, old_ref, sym_ref, link_ref, own_ref, next_sym_ref, *refs
):
    next_link_ref = None if last else refs[0]
    (
    got_ref, a_ref, p_ref, q_ref, z_ref, v_ref, inv_ref, ds, dr, gs, gr,
    ) = refs if last else refs[1:]
    i, y, c = place()
    chips, other = near()
    o = y * 2 + c
    n = z_ref.shape[0]
    down = (along(i, -stride), o)
    up = (along(i, stride), o)
    enter(chips + [other, down, up])
    copies, gathers = corrections(
        old_ref, sym_ref, got_ref, a_ref, own_ref, down, up, o, ds, dr, gs, gr
    )
    moved = [
        remote(link_ref.at[0], p_ref.at[o], ds.at[4], dr.at[4], up),
        remote(link_ref.at[1], q_ref.at[o], ds.at[5], dr.at[5], down),
    ]
    for copy in moved:
        copy.start()
    p_link = Gather(p_ref, gs.at[HALVES], gr.at[HALVES])
    q_link = Gather(q_ref, gs.at[HALVES + 1], gr.at[HALVES + 1])
    collect(z_ref, a_ref, gathers)

    def begin_links():
        for copy, link in zip(moved, (p_link, q_link)):
            copy.wait_recv()
            link.start()

    late = stride == 2
    if not late:
        begin_links()
    half = v_ref.at[:n]

    def between(k):
        if k == 0 and late:
            begin_links()
        if k == 1 and not late:
            p_link.forward()
        if k == 2:
            if late:
                p_link.forward()
            p_link.finish()
            v_ref[:n] = p_ref[...].reshape(n, n)
            for step in range(3):
                solve_step(half, z_ref, inv_ref, step)
            if not late:
                q_link.forward()
        if k == 3:
            if late:
                q_link.forward()
            q_link.finish()
            v_ref[n:] = q_ref[...].reshape(n, n)
            for step in range(3):
                solve_step(v_ref, z_ref, inv_ref, step, n)
            solve_step(v_ref, z_ref, inv_ref, 3)

    factor(z_ref, inv_ref, between)
    products(v_ref, next_sym_ref, next_link_ref, o)
    for copy in copies + moved:
        copy.wait_send()
    for gather in gathers + [p_link, q_link]:
        gather.close()


def final_kernel(
    stride, old_ref, sym_ref, l_ref, got_ref, a_ref, z_ref, inv_ref, ds, dr, gs, gr
):
    i, y, c = place()
    chips, other = near()
    o = y * 2 + c
    n = z_ref.shape[0]
    down = (along(i, -stride), o)
    up = (along(i, stride), o)
    enter(chips + [other, down, up])
    copies, gathers = corrections(
        old_ref, sym_ref, got_ref, a_ref, None, down, up, o, ds, dr, gs, gr
    )
    collect(z_ref, a_ref, gathers)
    factor(z_ref, inv_ref)
    row = lax.broadcasted_iota(jnp.int32, (n, n), 0)
    col = lax.broadcasted_iota(jnp.int32, (n, n), 1)
    l_ref[...] = jnp.where(col <= row, z_ref[...], 0.0)
    for copy in copies:
        copy.wait_send()
    for gather in gathers:
        gather.close()


VMEM = pl.BlockSpec(memory_space=pltpu.VMEM)
SMEM = pl.BlockSpec(memory_space=pltpu.SMEM)
DMA = pltpu.SemaphoreType.DMA


def f32(*shape):
    return jax.ShapeDtypeStruct(shape, jnp.float32)


def scratch(*shape):
    return pltpu.VMEM(shape, jnp.float32)


def call(kernel, out_shape, in_specs, scratch_shapes=(), collective_id=None):
    extra = {}
    if collective_id is not None:
        extra = dict(collective_id=collective_id, has_side_effects=True)
    return pl.pallas_call(
        kernel,
        out_shape=out_shape,
        in_specs=in_specs,
        out_specs=jax.tree.map(lambda _: VMEM, out_shape),
        scratch_shapes=scratch_shapes,
        compiler_params=pltpu.CompilerParams(vmem_limit_bytes=VMEM_LIMIT, **extra),
    )


def per_device(basis, obs_weight, col_pattern, tile_block, spatial_prec, time_coef):
    segments = lax.axis_size("tm")
    copies = lax.axis_size("obs")
    n = spatial_prec.shape[0]
    part = n // copies
    piece = (ROWS, WIDE)
    hops = 2 * CHIPS - 1

    grams = call(
        scaled_tiles_gram,
        f32(TB_DEV, CHIPS, 2, *piece),
        [VMEM, VMEM, SMEM, SMEM],
    )(basis, obs_weight, col_pattern, tile_block)
    blocks = scratch(n // BLK, BLK, BLK)
    pieces = scratch(HALVES, SLOTS, HALF, WIDE)
    middle, gram1 = call(
        segment_kernel,
        (f32(n, n), f32(*piece)),
        [SMEM, VMEM, VMEM],
        [
            pieces,
            scratch(TB_DEV, CHIPS, *piece),
            scratch(TB_DEV, CHIPS, *piece),
            scratch(TB_DEV, CHIPS - 1, *piece),
            scratch(n, n),
            scratch(n, n),
            blocks,
            DMA((HALVES + 1,)),
            DMA((HALVES + 1,)),
            DMA((HALVES + 1, CHIPS - 1)),
            DMA((HALVES + 1, CHIPS - 1)),
            DMA((HALVES, hops)),
            DMA((HALVES, hops)),
        ],
        collective_id=1,
    )(time_coef, spatial_prec, grams)

    results = (f32(*piece), f32(2, *piece), f32(2, part, n))
    work = [scratch(n, n), scratch(2 * n, n), blocks]
    slabs = scratch(copies, part, n)
    own_piece, sym, link = call(
        first_level_kernel,
        results,
        [SMEM, VMEM, VMEM, VMEM],
        [scratch(*piece), scratch(*piece), pieces, slabs, *work]
        + [DMA((HALVES + 1,)), DMA((HALVES + 1,))]
        + [DMA((HALVES + 1, hops)), DMA((HALVES + 1, hops))],
        collective_id=2,
    )(time_coef, spatial_prec, middle, gram1)

    stride = 1
    while 2 * stride < segments:
        last = 4 * stride >= segments
        own_piece, sym, *more = call(
            functools.partial(level_kernel, stride, last),
            results[:2] if last else results,
            [VMEM, VMEM, VMEM],
            [scratch(2, *piece), pieces, slabs, slabs, *work]
            + [DMA((6,)), DMA((6,)), DMA((HALVES + 2, hops)), DMA((HALVES + 2, hops))],
            collective_id=2 + stride,
        )(own_piece, sym, link)
        link = more[0] if more else None
        stride = 2 * stride

    factor_out = call(
        functools.partial(final_kernel, stride),
        f32(n, n),
        [VMEM, VMEM],
        [scratch(2, *piece), pieces, scratch(n, n), blocks]
        + [DMA((4,)), DMA((4,)), DMA((HALVES, hops)), DMA((HALVES, hops))],
        collective_id=2 + stride,
    )(own_piece, sym)
    return factor_out[None]


def solution(mesh):
    in_specs = (
        P(("tm", "obs"), None, None),
        P(("tm", "obs"), None),
        P(("tm", "obs"), None),
        P(("tm", "obs")),
        P(),
        P(),
    )
    out_specs = P("tm", None, None)
    return jax.shard_map(
        per_device, mesh=mesh, in_specs=in_specs, out_specs=out_specs, check_vma=False
    )
```

```python
import functools

import jax
import jax.numpy as jnp
from jax import lax
from jax.experimental import pallas as pl
from jax.experimental.pallas import tpu as pltpu
from jax.sharding import PartitionSpec as P

CT = 128
TB_DEV = 2
BLK = 128
AT_ONCE = 4
VMEM_LIMIT = 48 * 1024 * 1024


def sub_bcast(x, k):
    return jnp.broadcast_to(x[k : k + 1, :], (8, BLK))


def lane_bcast(x, c):
    return jnp.broadcast_to(x[:, c : c + 1], (8, BLK))


def inverse_factor(rest):
    lane = lax.broadcasted_iota(jnp.int32, (8, BLK), 1)
    sub = lax.broadcasted_iota(jnp.int32, (8, BLK), 0)
    rows = []
    groups = BLK // 8
    for g in range(groups):
        own = rest[:8]
        cols = [lane_bcast(own, 8 * g + k) for k in range(8)]
        in_panel = (lane >= 8 * g) & (lane < 8 * g + 8)
        eye = (lane - 8 * g == sub).astype(jnp.float32)
        unit = jnp.where(in_panel, eye, own)
        full = unit
        scale = jnp.zeros((8, BLK), jnp.float32)
        for k in range(0, 8, 2):
            b0, b1 = cols[k], cols[k + 1]
            p, q, r = sub_bcast(b0, k), sub_bcast(b0, k + 1), sub_bcast(b1, k + 1)
            det = p * r - q * q
            inv = 1.0 / det
            m0 = (b0 * r - b1 * q) * inv
            m1 = (b1 * p - b0 * q) * inv
            qi = q * inv
            first, second = sub == k, sub == k + 1
            pair = first | second
            f0 = jnp.where(first, -(r * inv), jnp.where(second, qi, m0))
            f1 = jnp.where(first, qi, jnp.where(second, -(p * inv), m1))
            for j in range(k + 2, 8):
                cols[j] = (
                    jnp.where(pair, 0.0, cols[j])
                    - f0 * sub_bcast(cols[j], k)
                    - f1 * sub_bcast(cols[j], k + 1)
                )
            if g < groups - 1:
                full = (
                    jnp.where(pair, 0.0, full)
                    - f0 * sub_bcast(full, k)
                    - f1 * sub_bcast(full, k + 1)
                )
            ip = 1.0 / p
            below = sub > k + 1
            n0 = jnp.where(below, m0, jnp.where(second, q * ip, 0.0))
            n1 = jnp.where(below, m1, 0.0)
            unit = unit - n0 * sub_bcast(unit, k) - n1 * sub_bcast(unit, k + 1)
            scale = jnp.where(
                first, lax.rsqrt(p), jnp.where(second, lax.rsqrt(det * ip), scale)
            )
        rows.append(unit * scale)
        if g < groups - 1:
            rest = rest[8:]
            near, far = rest[:8], rest[8:]
            t = [lane_bcast(near, 8 * g + k) * sub_bcast(full, k) for k in range(8)]
            near = jnp.where(in_panel, 0.0, near) - (
                ((t[0] + t[1]) + (t[2] + t[3])) + ((t[4] + t[5]) + (t[6] + t[7]))
            )
            if g < groups - 2:
                zeros = jnp.zeros((8, BLK), jnp.float32)
                spread = jnp.concatenate(
                    [full if h == g else zeros for h in range(groups)], axis=0
                )
                hi, lo = split(spread)
                wide = lax.broadcasted_iota(jnp.int32, far.shape, 1)
                passed = (wide >= 8 * g) & (wide < 8 * g + 8)
                update = lax.dot_general(
                    as_left(far),
                    jnp.concatenate([hi, hi, lo], axis=0),
                    (((1,), (0,)), ((), ())),
                    preferred_element_type=jnp.float32,
                )
                far = jnp.where(passed, 0.0, far) - update
                rest = jnp.concatenate([near, far], axis=0)
            else:
                rest = near
    return rows


def split(x):
    hi = x.astype(jnp.bfloat16)
    return hi, (x - hi.astype(jnp.float32)).astype(jnp.bfloat16)


def as_left(x):
    hi, lo = split(x)
    return jnp.concatenate([hi, lo, hi], axis=1)


def as_right(x):
    hi, lo = split(x)
    return jnp.concatenate([hi, hi, lo], axis=1)


def dot_nt(left, right):
    return lax.dot_general(
        left, right, (((1,), (1,)), ((), ())), preferred_element_type=jnp.float32
    )


def factor(z_ref, inv_ref, between=None):
    lane = lax.broadcasted_iota(jnp.int32, (8, BLK), 1)
    sub = lax.broadcasted_iota(jnp.int32, (8, BLK), 0)
    steps = z_ref.shape[0] // BLK
    for k in range(steps):
        c = k * BLK
        rows = inverse_factor(z_ref[c : c + BLK, c : c + BLK])
        for g, row in enumerate(rows):
            inv_ref[k, 8 * g : 8 * g + 8, :] = jnp.where(lane <= sub + 8 * g, row, 0.0)
        column = dot_nt(as_left(z_ref[c:, c : c + BLK]), as_right(inv_ref[k]))
        z_ref[c:, c : c + BLK] = column
        if k < steps - 1:
            left, right = as_left(column[BLK:]), as_right(column[BLK:])
            for b in range(c + BLK, z_ref.shape[0], BLK):
                r = b - c - BLK
                z_ref[b:, b : b + BLK] -= dot_nt(left[r:], right[r : r + BLK])
        if between is not None:
            between(k)


def solve_step(v_ref, z_ref, inv_ref, k, first=0):
    c = k * BLK
    column = dot_nt(as_left(v_ref[first:, c : c + BLK]), as_right(inv_ref[k]))
    v_ref[first:, c : c + BLK] = column
    if c + BLK < z_ref.shape[0]:
        v_ref[first:, c + BLK :] -= dot_nt(
            as_left(column), as_right(z_ref[c + BLK :, c : c + BLK])
        )


SLOTS = 8
ROWS = 32
WIDE = 640


def split_at(s):
    return (s // 4 + 1) * BLK


def pack(top, bottom, s):
    def piece(w):
        return jnp.concatenate([top[:, :w], bottom[:, : WIDE - w]], axis=1)

    return jnp.where(s < 4, piece(BLK), piece(2 * BLK))


def pack_rows(ref, s):
    top = ref[pl.ds(pl.multiple_of(s * ROWS, ROWS), ROWS), :]
    bottom = ref[pl.ds(pl.multiple_of((2 * SLOTS - 1 - s) * ROWS, ROWS), ROWS), :]
    return pack(top, bottom, s)


HALVES = 2
HALF = ROWS // HALVES


def half_rows(h):
    return slice(h * HALF, (h + 1) * HALF)


def collect(z_ref, packed_ref, gathers):
    for gather in gathers:
        gather.forward()
    for h in range(HALVES):
        gathers[h].finish()
        for s in range(SLOTS):
            w = split_at(s)
            top = s * ROWS + h * HALF
            bottom = (2 * SLOTS - 1 - s) * ROWS + h * HALF
            z_ref[top : top + HALF, :w] = packed_ref[h, s, :, :w]
            z_ref[bottom : bottom + HALF, : WIDE - w] = packed_ref[h, s, :, w:]


def scaled_tiles_gram(basis_ref, weight_ref, tile_ref, out_ref, tiles_ref, sems):
    tiles, _, columns = basis_ref.shape
    loads = []
    for j in range(tiles // AT_ONCE):
        some = slice(j * AT_ONCE, (j + 1) * AT_ONCE)
        loads.append(
            pltpu.make_async_copy(basis_ref.at[some], tiles_ref.at[some], sems.at[j])
        )
        loads[j].start()
    root = jnp.sqrt(weight_ref[...]).T
    lane = lax.broadcasted_iota(jnp.int32, (1, columns), 1) // CT
    out_ref[...] = jnp.zeros_like(out_ref)
    for t in range(tiles):
        if t % AT_ONCE == 0:
            loads[t // AT_ONCE].wait()
        mask = jnp.zeros((1, columns), jnp.float32)
        for j in range(columns // CT):
            mask = jnp.where(lane == j, tile_ref[t, j].astype(jnp.float32), mask)
        raw = tiles_ref[t].astype(jnp.float32) * mask
        x = (root[:, t : t + 1] * raw).astype(jnp.bfloat16)
        gram = lax.dot_general(
            x, x, (((0,), (0,)), ((), ())), preferred_element_type=jnp.float32
        )
        m = lax.rem(tile_ref[t, columns // CT], TB_DEV)
        for s in range(SLOTS):
            w = split_at(s)
            r = (2 * SLOTS - 1 - s) * ROWS
            out_ref[m, s // 2, s % 2, :, :w] += gram[s * ROWS : (s + 1) * ROWS, :w]
            out_ref[m, s // 2, s % 2, :, w:] += gram[r : r + ROWS, : WIDE - w]


def place():
    where = lax.axis_index("obs")
    return lax.axis_index("tm"), where // 2, lax.rem(where, 2)


def enter(devices):
    barrier = pltpu.get_barrier_semaphore()
    for device in devices:
        pl.semaphore_signal(
            barrier, inc=1, device_id=device, device_id_type=pl.DeviceIdType.MESH
        )
    pl.semaphore_wait(barrier, len(devices))


def remote(src, dst, send, recv, device):
    return pltpu.make_async_remote_copy(
        src_ref=src,
        dst_ref=dst,
        send_sem=send,
        recv_sem=recv,
        device_id=device,
        device_id_type=pl.DeviceIdType.MESH,
    )


CHIPS = 4


def near():
    i, y, c = place()
    chips = [(i, lax.rem(y + d, CHIPS) * 2 + c) for d in range(1, CHIPS)]
    return chips, (i, y * 2 + 1 - c)


class Gather:
    def __init__(self, ref, send, recv):
        _, y, c = place()
        chips, other = near()
        own = ref.at[y * 2 + c]
        self.out = [
            remote(own, own, send.at[d], recv.at[d], chips[d]) for d in range(CHIPS - 1)
        ]
        self.cross, self.back = [], []
        for d in range(CHIPS):
            from_chip = lax.rem(y + CHIPS - d, CHIPS) * 2
            mine, theirs = ref.at[from_chip + c], ref.at[from_chip + 1 - c]
            sems = send.at[CHIPS - 1 + d], recv.at[CHIPS - 1 + d]
            self.cross.append(remote(mine, mine, *sems, other))
            self.back.append(remote(theirs, theirs, *sems, other))
        self.arrive = [
            remote(
                ref.at[lax.rem(y + CHIPS - d, CHIPS) * 2 + c],
                ref.at[lax.rem(y + CHIPS - d, CHIPS) * 2 + c],
                send.at[d - 1],
                recv.at[d - 1],
                chips[d - 1],
            )
            for d in range(1, CHIPS)
        ]

    def start(self):
        for copy in self.out:
            copy.start()
        self.cross[0].start()

    def forward(self):
        for d in (1, 3, 2):
            self.arrive[d - 1].wait_recv()
            self.cross[d].start()

    def finish(self):
        for copy in self.back:
            copy.wait_recv()

    def close(self):
        for copy in self.out + self.cross:
            copy.wait_send()


def share(ref, send, recv):
    return [Gather(ref.at[h], send.at[h], recv.at[h]) for h in range(HALVES)]


def rates(coef_ref):
    i, _, _ = place()
    count, last = coef_ref.shape[0], lax.axis_size("tm") - 1
    first = i * TB_DEV
    before = jnp.where(i > 0, coef_ref[lax.rem(first + count - 1, count)], 0.0)
    rate0, rate1 = coef_ref[first], coef_ref[first + 1]
    return before, rate0, rate1, jnp.where(i < last, rate1, 0.0), coef_ref[lax.rem(first + 2, count)]


def along(i, distance):
    count = lax.axis_size("tm")
    return lax.rem(i + count + distance, count)


def segment_kernel(
    coef_ref, s_ref, part_ref, m_ref, second_ref,
    first_ref, other_ref, sum_ref, got_ref, z_ref, v_ref, inv_ref, xs, xr, ss, sr, gs, gr,
):
    i, y, c = place()
    chips, other = near()
    enter(chips + [other])
    parts = [(0, half_rows(0)), (0, half_rows(1)), (1, slice(0, ROWS))]
    swap = [
        remote(part_ref.at[t, :, 1 - c, r], other_ref.at[t, :, r], xs.at[j], xr.at[j], other)
        for j, (t, r) in enumerate(parts)
    ]
    spread = [
        [
            remote(
                sum_ref.at[t, lax.rem(y + d, CHIPS), r],
                got_ref.at[t, d - 1, r],
                ss.at[j, d - 1],
                sr.at[j, d - 1],
                chips[d - 1],
            )
            for d in range(1, CHIPS)
        ]
        for j, (t, r) in enumerate(parts)
    ]
    gathers = share(first_ref, gs, gr)

    def chip_sum(j):
        t, r = parts[j]
        swap[j].wait_recv()
        sum_ref[t, :, r] = part_ref[t, :, c, r] + other_ref[t, :, r]

    def total(j):
        t, r = parts[j]
        for copy in spread[j]:
            copy.wait_recv()
        return (sum_ref[t, y, r] + got_ref[t, 0, r]) + (got_ref[t, 1, r] + got_ref[t, 2, r])

    for copy in swap:
        copy.start()
    for h in range(HALVES):
        chip_sum(h)
        for copy in spread[h]:
            copy.start()
    v_ref[...] = s_ref[...]
    for h in range(HALVES):
        first_ref[h, y * 2 + c] = total(h)
        gathers[h].start()
    chip_sum(2)
    collect(z_ref, first_ref, gathers)
    for copy in spread[2]:
        copy.start()
    _, rate0, _, _, _ = rates(coef_ref)
    z_ref[...] += (1.0 + rate0 * rate0) * s_ref[...]

    def between(k):
        if k == 2:
            second_ref[...] = total(2)
        solve_step(v_ref, z_ref, inv_ref, k)

    factor(z_ref, inv_ref, between)
    solved = v_ref[...]
    m_ref[...] = dot_nt(as_left(solved), as_right(solved))
    for copy in swap + spread[0] + spread[1] + spread[2]:
        copy.wait_send()
    for gather in gathers:
        gather.close()


def products(v_ref, sym_ref, link_ref, o):
    n = v_ref.shape[1]
    p, q = as_right(v_ref[:n]), as_right(v_ref[n:])

    def rows(first, count):
        return v_ref[pl.ds(pl.multiple_of(first, count), count), :]

    for t, right in enumerate((p, q)):
        left = [
            rows(t * n + o * ROWS, ROWS),
            rows(t * n + (2 * SLOTS - 1 - o) * ROWS, ROWS),
        ]
        if link_ref is not None:
            part = link_ref.shape[1]
            left.append(rows((1 - t) * n + o * part, part))
        both = dot_nt(as_left(jnp.concatenate(left, axis=0)), right)
        sym_ref[t] = pack(both[:ROWS], both[ROWS : 2 * ROWS], o)
        if link_ref is not None:
            link_ref[1 - t] = -both[2 * ROWS :]


def first_level_kernel(
    coef_ref, s_ref, m_ref, g_ref, own_ref, sym_ref, link_ref,
    mine_ref, got_ref, a_ref, above_ref, z_ref, v_ref, inv_ref, ds, dr, gs, gr,
):
    i, y, c = place()
    chips, other = near()
    o = y * 2 + c
    n = z_ref.shape[0]
    part = above_ref.shape[1]
    down = (along(i, -1), o)
    up = (along(i, 1), o)
    enter(chips + [other, down, up])
    mine = pack_rows(m_ref, o)
    mine_ref[...] = mine
    own = m_ref.at[pl.ds(pl.multiple_of(o * part, part), part)]
    pieces = [
        remote(mine_ref.at[half_rows(h)], got_ref.at[half_rows(h)], ds.at[h], dr.at[h], down)
        for h in range(HALVES)
    ]
    whole = remote(own, above_ref.at[o], ds.at[HALVES], dr.at[HALVES], down)
    for copy in pieces:
        copy.start()
    gathers = share(a_ref, gs, gr)
    gather_above = Gather(above_ref, gs.at[HALVES], gr.at[HALVES])
    before, rate0, rate1, up1, rate2 = rates(coef_ref)
    rows = (1.0 + rate1 * rate1) * pack_rows(s_ref, o) + g_ref[...] - (rate0 * rate0) * mine
    own_ref[...] = rows
    for h in range(HALVES):
        r = half_rows(h)
        pieces[h].wait_recv()
        part_rows = own_ref[r] - (up1 * up1) * got_ref[r]
        own_ref[r] = part_rows
        a_ref[h, o] = part_rows
        gathers[h].start()
    whole.start()
    v_ref[:n] = -(before * rate0) * m_ref[...]
    collect(z_ref, a_ref, gathers)
    whole.wait_recv()
    gather_above.start()
    half = v_ref.at[:n]

    def between(k):
        if k < 3:
            solve_step(half, z_ref, inv_ref, k)
        else:
            solve_step(v_ref, z_ref, inv_ref, k)
        if k == 1:
            gather_above.forward()
        if k == 2:
            gather_above.finish()
            v_ref[n:] = -(up1 * rate2) * above_ref[...].reshape(n, n)
            for step in range(3):
                solve_step(v_ref, z_ref, inv_ref, step, n)

    factor(z_ref, inv_ref, between)
    products(v_ref, sym_ref, link_ref, o)
    for copy in pieces + [whole]:
        copy.wait_send()
    for gather in gathers + [gather_above]:
        gather.close()


def corrections(old_ref, sym_ref, got_ref, a_ref, own_ref, down, up, o, ds, dr, gs, gr):
    copies = [
        [
            remote(
                sym_ref.at[t, half_rows(h)],
                got_ref.at[t, half_rows(h)],
                ds.at[2 * h + t],
                dr.at[2 * h + t],
                device,
            )
            for t, device in enumerate((down, up))
        ]
        for h in range(HALVES)
    ]
    for pair in copies:
        for copy in pair:
            copy.start()
    gathers = share(a_ref, gs, gr)
    for h, pair in enumerate(copies):
        r = half_rows(h)
        for copy in pair:
            copy.wait_recv()
        rows = old_ref[r] - got_ref[0, r] - got_ref[1, r]
        if own_ref is not None:
            own_ref[r] = rows
        a_ref[h, o] = rows
        gathers[h].start()
    return copies[0] + copies[1], gathers


def level_kernel(
    stride, last, old_ref, sym_ref, link_ref, own_ref, next_sym_ref, *refs
):
    next_link_ref = None if last else refs[0]
    (
    got_ref, a_ref, p_ref, q_ref, z_ref, v_ref, inv_ref, ds, dr, gs, gr,
    ) = refs if last else refs[1:]
    i, y, c = place()
    chips, other = near()
    o = y * 2 + c
    n = z_ref.shape[0]
    down = (along(i, -stride), o)
    up = (along(i, stride), o)
    enter(chips + [other, down, up])
    copies, gathers = corrections(
        old_ref, sym_ref, got_ref, a_ref, own_ref, down, up, o, ds, dr, gs, gr
    )
    moved = [
        remote(link_ref.at[0], p_ref.at[o], ds.at[4], dr.at[4], up),
        remote(link_ref.at[1], q_ref.at[o], ds.at[5], dr.at[5], down),
    ]
    for copy in moved:
        copy.start()
    p_link = Gather(p_ref, gs.at[HALVES], gr.at[HALVES])
    q_link = Gather(q_ref, gs.at[HALVES + 1], gr.at[HALVES + 1])
    collect(z_ref, a_ref, gathers)

    def begin_links():
        for copy, link in zip(moved, (p_link, q_link)):
            copy.wait_recv()
            link.start()

    late = stride == 2
    if not late:
        begin_links()
    half = v_ref.at[:n]

    def between(k):
        if k == 0 and late:
            begin_links()
        if k == 1 and not late:
            p_link.forward()
        if k == 2:
            if late:
                p_link.forward()
            p_link.finish()
            v_ref[:n] = p_ref[...].reshape(n, n)
            for step in range(3):
                solve_step(half, z_ref, inv_ref, step)
            if not late:
                q_link.forward()
        if k == 3:
            if late:
                q_link.forward()
            q_link.finish()
            v_ref[n:] = q_ref[...].reshape(n, n)
            for step in range(3):
                solve_step(v_ref, z_ref, inv_ref, step, n)
            solve_step(v_ref, z_ref, inv_ref, 3)

    factor(z_ref, inv_ref, between)
    products(v_ref, next_sym_ref, next_link_ref, o)
    for copy in copies + moved:
        copy.wait_send()
    for gather in gathers + [p_link, q_link]:
        gather.close()


def final_kernel(
    stride, old_ref, sym_ref, l_ref, got_ref, a_ref, z_ref, inv_ref, ds, dr, gs, gr
):
    i, y, c = place()
    chips, other = near()
    o = y * 2 + c
    n = z_ref.shape[0]
    down = (along(i, -stride), o)
    up = (along(i, stride), o)
    enter(chips + [other, down, up])
    copies, gathers = corrections(
        old_ref, sym_ref, got_ref, a_ref, None, down, up, o, ds, dr, gs, gr
    )
    collect(z_ref, a_ref, gathers)
    factor(z_ref, inv_ref)
    row = lax.broadcasted_iota(jnp.int32, (n, n), 0)
    col = lax.broadcasted_iota(jnp.int32, (n, n), 1)
    l_ref[...] = jnp.where(col <= row, z_ref[...], 0.0)
    for copy in copies:
        copy.wait_send()
    for gather in gathers:
        gather.close()


VMEM = pl.BlockSpec(memory_space=pltpu.VMEM)
SMEM = pl.BlockSpec(memory_space=pltpu.SMEM)
DMA = pltpu.SemaphoreType.DMA


def f32(*shape):
    return jax.ShapeDtypeStruct(shape, jnp.float32)


def scratch(*shape):
    return pltpu.VMEM(shape, jnp.float32)


def call(kernel, out_shape, in_specs, scratch_shapes=(), collective_id=None):
    extra = {}
    if collective_id is not None:
        extra = dict(collective_id=collective_id, has_side_effects=True)
    return pl.pallas_call(
        kernel,
        out_shape=out_shape,
        in_specs=in_specs,
        out_specs=jax.tree.map(lambda _: VMEM, out_shape),
        scratch_shapes=scratch_shapes,
        compiler_params=pltpu.CompilerParams(vmem_limit_bytes=VMEM_LIMIT, **extra),
    )


def per_device(basis, obs_weight, col_pattern, tile_block, spatial_prec, time_coef):
    segments = lax.axis_size("tm")
    copies = lax.axis_size("obs")
    n = spatial_prec.shape[0]
    part = n // copies
    piece = (ROWS, WIDE)
    hops = 2 * CHIPS - 1

    grams = call(
        scaled_tiles_gram,
        f32(TB_DEV, CHIPS, 2, *piece),
        [pl.BlockSpec(memory_space=pl.ANY), VMEM, SMEM],
        [pltpu.VMEM(basis.shape, basis.dtype), DMA((basis.shape[0] // AT_ONCE,))],
    )(basis, obs_weight, jnp.concatenate([col_pattern, tile_block[:, None]], axis=1))
    blocks = scratch(n // BLK, BLK, BLK)
    pieces = scratch(HALVES, SLOTS, HALF, WIDE)
    middle, gram1 = call(
        segment_kernel,
        (f32(n, n), f32(*piece)),
        [SMEM, VMEM, VMEM],
        [
            pieces,
            scratch(TB_DEV, CHIPS, *piece),
            scratch(TB_DEV, CHIPS, *piece),
            scratch(TB_DEV, CHIPS - 1, *piece),
            scratch(n, n),
            scratch(n, n),
            blocks,
            DMA((HALVES + 1,)),
            DMA((HALVES + 1,)),
            DMA((HALVES + 1, CHIPS - 1)),
            DMA((HALVES + 1, CHIPS - 1)),
            DMA((HALVES, hops)),
            DMA((HALVES, hops)),
        ],
        collective_id=1,
    )(time_coef, spatial_prec, grams)

    results = (f32(*piece), f32(2, *piece), f32(2, part, n))
    work = [scratch(n, n), scratch(2 * n, n), blocks]
    slabs = scratch(copies, part, n)
    own_piece, sym, link = call(
        first_level_kernel,
        results,
        [SMEM, VMEM, VMEM, VMEM],
        [scratch(*piece), scratch(*piece), pieces, slabs, *work]
        + [DMA((HALVES + 1,)), DMA((HALVES + 1,))]
        + [DMA((HALVES + 1, hops)), DMA((HALVES + 1, hops))],
        collective_id=2,
    )(time_coef, spatial_prec, middle, gram1)

    stride = 1
    while 2 * stride < segments:
        last = 4 * stride >= segments
        own_piece, sym, *more = call(
            functools.partial(level_kernel, stride, last),
            results[:2] if last else results,
            [VMEM, VMEM, VMEM],
            [scratch(2, *piece), pieces, slabs, slabs, *work]
            + [DMA((6,)), DMA((6,)), DMA((HALVES + 2, hops)), DMA((HALVES + 2, hops))],
            collective_id=2 + stride,
        )(own_piece, sym, link)
        link = more[0] if more else None
        stride = 2 * stride

    factor_out = call(
        functools.partial(final_kernel, stride),
        f32(n, n),
        [VMEM, VMEM],
        [scratch(2, *piece), pieces, scratch(n, n), blocks]
        + [DMA((4,)), DMA((4,)), DMA((HALVES, hops)), DMA((HALVES, hops))],
        collective_id=2 + stride,
    )(own_piece, sym)
    return factor_out[None]


def solution(mesh):
    in_specs = (
        P(("tm", "obs"), None, None),
        P(("tm", "obs"), None),
        P(("tm", "obs"), None),
        P(("tm", "obs")),
        P(),
        P(),
    )
    out_specs = P("tm", None, None)
    return jax.shard_map(
        per_device, mesh=mesh, in_specs=in_specs, out_specs=out_specs, check_vma=False
    )
```
